256 devices in a mesh: row: 16 (over y, z_hi), col: 16 (over x, z_lo, core).
Axes of the slice: x: 4, y: 4, z: 8 (z_hi: 4, z_lo: 2; z = z_hi * 2 + z_lo), core: 2. Of those that a mesh axis runs over, the one named last changes fastest.
Arguments:
- amplitudes: bfloat16 [16, 16, 1, 16, 16, 1, 4096], P('row', None, None, None, 'col'), may hold values from -6 to 6
- panels: bfloat16 [256, 64, 4096], P(('row', 'col')), may hold values from -0.75 to 0.75
- fock_virt: bfloat16 [64, 64], replicated, may hold values from -0.75 to 0.75
- occ_energy: float32 [256], replicated, may hold values from -2 to -0.5
- strong_pairs: int32 [16, 16, 1, 16, 16, 1], P('row', None, None, None, 'col'), may hold values from 0 to 1, as said below
Outputs:
- sym_residual: bfloat16 [16, 16, 1, 16, 16, 1, 4096], P('row', None, None, None, 'col')
The draws below stay inside these ranges and needn't reach their ends.
Inputs may be any that keep to these rules, and one draw needn't show every extreme that they name: `strong_pairs`: flag[i, j] equals flag[j, i], and is 1 wherever |i - j| <= 2.
All inputs are finite; a program needn't handle non-finite values.
Results may differ from the reference program's by a relative error of at most 0.0049.
Values may be sent and summed in bfloat16 or wider, within the bound.
A program may use at most 128 MiB of HBM per device.

```python
import jax
import jax.numpy as jnp
from jax import lax

O = 256
VS = 64
NAUX = 4096
OF = 1
VV = 4096
N_ROW = 16
N_COL = 16


def draw_strong_pairs(key, part):
    key = jax.random.fold_in(key, 7)
    levels = jax.random.randint(key, (O, O), 0, 2, dtype=jnp.int32)
    orbital = jnp.arange(O, dtype=jnp.int32)
    upper = orbital[:, None] < orbital[None, :]
    chosen = jnp.where(upper, levels, levels.T)
    near = jnp.abs(orbital[:, None] - orbital[None, :]) <= 2
    kept = jnp.logical_or(near, chosen == 0).astype(jnp.int32)
    return kept.reshape(N_ROW, N_COL, OF, N_ROW, N_COL, OF)


def block_scale(key, extent, cuts, least, top_value):
    level, own = 1.0, jax.random.fold_in(key, 6)
    for axis_at, blocks in cuts:
        steps = jnp.exp(jax.random.uniform(jax.random.fold_in(own, axis_at), (blocks,), jnp.float32, least / len(cuts), top_value / len(cuts)))
        level = level * jnp.repeat(steps, extent[axis_at] // blocks).reshape([-1 if axis == axis_at else 1 for axis in range(len(extent))])
    return level


def bell_draw(rng, extent, deviation, reach, split=(), kind=jnp.bfloat16):
    array = deviation * jax.random.normal(rng, extent, jnp.float32)
    if split:
        array = array * block_scale(rng, extent, split, -0.22, 0.18)
    return jnp.clip(array, -reach, reach).astype(kind)


def setup_inputs(seed: int = 0) -> dict:
    arg_keys = jax.random.split(jax.random.key(seed), 6)
    return {
        "amplitudes": bell_draw(arg_keys[0], (N_ROW, N_COL, OF, N_ROW, N_COL, OF, VV), 1.0, 6.0, ((0, 16), (4, 16))),
        "panels": bell_draw(arg_keys[1], (O, VS, NAUX), (NAUX ** 0.5) ** -0.5, 0.75, ((0, 256),)),
        "fock_virt": bell_draw(arg_keys[2], (VS, VS), VS ** -0.5, 0.75),
        "occ_energy": jnp.clip(jax.random.uniform(arg_keys[3], (O,), jnp.float32, -2.0, -0.5), -2.0, -0.5),
        "strong_pairs": draw_strong_pairs(jax.random.fold_in(arg_keys[5], 71), 0),
    }


def reference(amplitudes, panels, fock_virt, occ_energy, strong_pairs):
    amp = amplitudes.reshape(O, O, VS, VS)
    flags = strong_pairs.reshape(O, O)
    flat_panels = panels.reshape(O * VS, NAUX)
    fock_wide = fock_virt.astype(jnp.float32)

    def row_residual(index):
        left = lax.dynamic_index_in_dim(panels, index, 0, keepdims=False)
        exch = jnp.dot(left, flat_panels.T, preferred_element_type=jnp.float32)
        exch = exch.reshape(VS, O, VS).transpose(1, 0, 2)
        tiles = lax.dynamic_index_in_dim(amp, index, 0, keepdims=False).astype(jnp.float32)
        first = jnp.einsum('ac,jcb->jab', fock_wide, tiles)
        second = jnp.einsum('jac,bc->jab', tiles, fock_wide)
        energy = lax.dynamic_index_in_dim(occ_energy, index, 0, keepdims=False) + occ_energy
        return (exch + first + second - energy[:, None, None] * tiles).astype(jnp.bfloat16)

    resid = lax.map(row_residual, jnp.arange(O, dtype=jnp.int32))

    def row_symmetric(index):
        own = lax.dynamic_index_in_dim(resid, index, 0, keepdims=False).astype(jnp.float32)
        mirror = lax.dynamic_index_in_dim(resid, index, 1, keepdims=False).transpose(0, 2, 1).astype(jnp.float32)
        weight = lax.dynamic_index_in_dim(flags, index, 0, keepdims=False).astype(jnp.float32)
        return (weight[:, None, None] * (own + mirror)).astype(jnp.bfloat16)

    result = lax.map(row_symmetric, jnp.arange(O, dtype=jnp.int32))
    return result.reshape(N_ROW, N_COL, OF, N_ROW, N_COL, OF, VV)
```

```python
import jax
import jax.numpy as jnp
from jax import lax
from jax.experimental import pallas as pl
from jax.experimental.pallas import tpu as pltpu
from jax.sharding import PartitionSpec as P

MESH = pl.DeviceIdType.MESH
F32 = jnp.float32
BF16 = jnp.bfloat16
N = 16
W = 64
NT = (((1,), (1,)), ((), ()))


def kernel(
    amp, panel, fock, occ, flags, out,
    left, right, tin, tsend, trecv, big, flat, obuf, diag,
    psem, tsem, tsend_sem, trecv_sem, own_sem, out_sem,
    lsend, lrecv, rsend, rrecv, ready,
):
    r = lax.axis_index("row")
    c = lax.axis_index("col")
    y, zh = r // 4, r % 4
    x, low = c // 4, c % 4

    def rows(dy, dz):
        return (y + dy + 4) % 4 * 4 + (zh + dz + 4) % 4

    def cols(dx):
        return (x + dx + 4) % 4 * 4 + low

    sib = c + 1 - 2 * (c % 2)
    zl_c = c + 2 - 4 * (low // 2)

    load_left = pltpu.make_async_copy(panel.at[0], left.at[c], psem.at[0])
    load_right = pltpu.make_async_copy(panel.at[0], right.at[r], psem.at[1])
    load_t = pltpu.make_async_copy(amp, tin, tsem)
    load_left.start()
    load_right.start()
    load_t.start()

    bar = pltpu.get_barrier_semaphore()

    def greet(i, carry):
        pl.semaphore_signal(bar, inc=1, device_id=(r, (c + i) % N), device_id_type=MESH)
        pl.semaphore_signal(bar, inc=1, device_id=((r + i) % N, c), device_id_type=MESH)
        return carry

    lax.fori_loop(1, N, greet, 0)

    spread = (
        lax.broadcasted_iota(jnp.int32, (256, W), 0) % W
        == lax.broadcasted_iota(jnp.int32, (256, W), 1)
    ).astype(BF16)
    wide = jnp.dot(spread, fock[...], preferred_element_type=F32).astype(BF16)
    wide = lax.dot_general(wide, spread, NT, preferred_element_type=F32)
    same = (
        lax.broadcasted_iota(jnp.int32, (256, 256), 0) // W
        == lax.broadcasted_iota(jnp.int32, (256, 256), 1) // W
    )
    diag[...] = jnp.where(same, wide, 0.0).astype(BF16)

    pl.semaphore_wait(bar, 2 * (N - 1))

    started = []

    def send_left(slot, col, k):
        cp = pltpu.make_async_remote_copy(
            src_ref=left.at[slot], dst_ref=left.at[slot],
            send_sem=lsend.at[k], recv_sem=lrecv.at[slot],
            device_id=(r, col), device_id_type=MESH,
        )
        cp.start()
        started.append(cp)

    def got_left(slot):
        pltpu.make_async_remote_copy(
            src_ref=left.at[slot], dst_ref=left.at[slot],
            send_sem=lsend.at[0], recv_sem=lrecv.at[slot],
            device_id=(r, sib), device_id_type=MESH,
        ).wait_recv()

    def half(slot, h):
        return right.at[slot, pl.ds(h * 32, 32)]

    def send_right(slot, h, row, k):
        cp = pltpu.make_async_remote_copy(
            src_ref=half(slot, h), dst_ref=half(slot, h),
            send_sem=rsend.at[k], recv_sem=rrecv.at[slot, h],
            device_id=(row, c), device_id_type=MESH,
        )
        cp.start()
        started.append(cp)

    def got_right(slot, h):
        pltpu.make_async_remote_copy(
            src_ref=half(slot, h), dst_ref=half(slot, h),
            send_sem=rsend.at[0], recv_sem=rrecv.at[slot, h],
            device_id=(rows(1, 0), c), device_id_type=MESH,
        ).wait_recv()

    up_z, down_z = rows(0, 1), rows(0, -1)
    up_y, down_y = rows(1, 0), rows(-1, 0)
    load_right.wait()
    send_right(r, 0, down_z, 0)
    send_right(r, 1, up_z, 1)
    send_right(r, 1, down_z, 2)
    send_right(r, 0, up_z, 3)
    load_left.wait()
    send_left(c, zl_c, 0)
    send_left(c, sib, 1)
    for h in range(2):
        send_right(r, h, up_y, 4 + 2 * h)
        send_right(r, h, down_y, 5 + 2 * h)
    send_left(c, cols(1), 2)
    send_left(c, cols(-1), 3)
    send_left(c, cols(2), 4)

    def all_in(i, carry):
        pl.semaphore_signal(ready, inc=1, device_id=((r + i) % N, c), device_id_type=MESH)
        return carry

    lax.fori_loop(1, N, all_in, 0)
    load_t.wait()
    pl.semaphore_wait(ready, N - 1)

    low_lanes = lax.broadcasted_iota(jnp.int32, (32, 128), 1) < W

    def pair_up(first, second):
        return (
            jnp.where(low_lanes, first, pltpu.roll(second, W, 1)),
            jnp.where(low_lanes, pltpu.roll(first, W, 1), second),
        )

    def spread_amp(step, carry):
        p = (c // 2 + step) % 8
        for f in range(2):
            ci = 2 * p + f
            for a in range(32):
                flat[ci, pl.ds(a * N, N), :] = tin[ci, :, pl.ds(a * 128, 128)].astype(F32)
            for q in range(8):
                even, odd = pair_up(
                    flat[ci, pl.ds(2 * q, 32, stride=N), :],
                    flat[ci, pl.ds(2 * q + 1, 32, stride=N), :],
                )
                big[q, pl.ds(ci * W, 32, stride=2), :] = even
                big[q, pl.ds(ci * W + 1, 32, stride=2), :] = odd
        for q in range(8):
            block = big[q, pl.ds(pl.multiple_of(p * 128, 128), 128), :].T
            for g in range(2):
                first, second = pair_up(
                    block[g * W : g * W + 32], block[g * W + 32 : g * W + W]
                )
                tsend[2 * p * N + 2 * q + g] = first.astype(BF16)
                tsend[(2 * p + 1) * N + 2 * q + g] = second.astype(BF16)

        def route(k, inner):
            rj = (r + k // 2) % N
            ci = 2 * p + k % 2

            @pl.when(jnp.logical_or(rj != r, ci != c))
            def _():
                pltpu.make_async_remote_copy(
                    src_ref=tsend.at[ci * N + rj], dst_ref=trecv.at[c * N + r],
                    send_sem=tsend_sem, recv_sem=trecv_sem,
                    device_id=(rj, ci), device_id_type=MESH,
                ).start()

            return inner

        lax.fori_loop(0, 2 * N, route, 0)
        return carry

    lax.fori_loop(0, 8, spread_amp, 0)
    own_tile = pltpu.make_async_copy(
        tsend.at[c * N + r], trecv.at[c * N + r], own_sem
    )
    own_tile.start()

    got_left(zl_c)
    send_left(zl_c, sib, 5)
    send_left(zl_c, cols(1), 6)
    send_left(zl_c, cols(-1), 7)
    send_left(zl_c, cols(2), 8)
    k = 8
    for slot, on, h in ((up_z, down_z, 0), (down_z, up_z, 1)):
        got_right(slot, h)
        send_right(slot, h, on, k)
        send_right(slot, h, up_y, k + 1)
        send_right(slot, h, down_y, k + 2)
        k += 3
    for slot, h in ((up_z, 1), (down_z, 0)):
        got_right(slot, h)
        send_right(slot, h, up_y, k)
        send_right(slot, h, down_y, k + 1)
        k += 2

    def pass_y(dz):
        nonlocal k
        got_right(rows(-1, dz), 0)
        send_right(rows(-1, dz), 0, up_y, k)
        got_right(rows(1, dz), 1)
        send_right(rows(1, dz), 1, down_y, k + 1)
        k += 2

    pass_y(0)
    kl = 9
    for dx in (1, -1):
        slot = cols(dx)
        got_left(slot)
        send_left(slot, sib, kl)
        kl += 1
    far_z = rows(0, 2)
    for h in range(2):
        got_right(far_z, h)
        send_right(far_z, h, up_y, k)
        send_right(far_z, h, down_y, k + 1)
        k += 2
    pass_y(1)
    pass_y(-1)
    other_zl = 2 - 4 * (low // 2)
    for slot in (cols(2), cols(1) + other_zl, cols(-1) + other_zl, cols(2) + other_zl):
        got_left(slot)
        send_left(slot, sib, kl)
        kl += 1
    pass_y(2)

    own_tile.wait()
    pltpu.make_async_copy(
        tsend.at[pl.ds(0, N * N - 1)], trecv.at[pl.ds(0, N * N - 1)], trecv_sem
    ).wait()

    def linear(step, carry):
        for f in range(4):
            ci = step * 4 + f
            for q in range(8):
                top, bottom = pair_up(
                    trecv[ci * N + 2 * q].astype(F32), trecv[ci * N + 2 * q + 1].astype(F32)
                )
                span = pl.ds(pl.multiple_of(ci * W, W), 32)
                big[q, span, :] = big[q, span, :] + top
                span = pl.ds(pl.multiple_of(ci * W + 32, 32), 32)
                big[q, span, :] = big[q, span, :] + bottom
        span = pl.ds(pl.multiple_of(step * 256, 256), 256)
        which = lax.broadcasted_iota(jnp.int32, (256, 256), 0) // W
        first_e = jnp.zeros((256, 256), F32)
        for f in range(4):
            first_e = jnp.where(which == f, occ[r * N + step * 4 + f], first_e)
        which = lax.broadcasted_iota(jnp.int32, (256, 256), 1) // W
        for g in range(4):
            s = jnp.concatenate([big[2 * g, span, :], big[2 * g + 1, span, :]], axis=1)
            energy = first_e
            for f in range(4):
                energy = energy + jnp.where(which == f, occ[(4 * g + f) * N + c], 0.0)
            sb = s.astype(BF16)
            total = jnp.dot(diag[...], sb, preferred_element_type=F32)
            total = total + lax.dot_general(sb, diag[...], NT, preferred_element_type=F32)
            total = total - energy * s
            big[2 * g, span, :] = total[:, :128]
            big[2 * g + 1, span, :] = total[:, 128:]
        return carry

    lax.fori_loop(0, 4, linear, 0)

    for xs in range(4):
        for b in range(2):
            got_left(xs * 4 + b * 2 + 1 - c % 2)

    def group(dy):
        g = (y + dy + 4) % 4
        block = right.at[pl.ds(pl.multiple_of(g * 4, 4), 4)]

        def part(step, carry):
            span = pl.ds(pl.multiple_of(step * 256, 256), 256)
            lhs = left[pl.ds(step * 4, 4)].reshape(256, 4096)
            rhs = block[...].reshape(256, 4096)
            exch = lax.dot_general(lhs, rhs, NT, preferred_element_type=F32)
            for q in range(2):
                big[2 * g + q, span, :] = (
                    big[2 * g + q, span, :] + 2.0 * exch[:, q * 128 : q * 128 + 128]
                )
            for f in range(4):
                ci = step * 4 + f
                for q in range(2):
                    rj = 4 * g + 2 * q
                    even = big[2 * g + q, pl.ds(ci * W, 32, stride=2), :]
                    odd = big[2 * g + q, pl.ds(ci * W + 1, 32, stride=2), :]
                    one, two = pair_up(even, odd)
                    flat[ci, pl.ds(rj, 32, stride=N), :] = one * flags[ci, rj].astype(F32)
                    flat[ci, pl.ds(rj + 1, 32, stride=N), :] = (
                        two * flags[ci, rj + 1].astype(F32)
                    )
            return carry

        lax.fori_loop(0, 4, part, 0)

    group(0)
    for dy, h in ((1, 0), (-1, 1)):
        for dz in (0, 1, -1, 2):
            got_right(rows(dy, dz), h)
        group(dy)
    for h in range(2):
        for dz in (0, 1, -1, 2):
            got_right(rows(2, dz), h)
    group(2)

    def finish(ci, carry):
        for a in range(32):
            obuf[ci, :, pl.ds(a * 128, 128)] = flat[ci, pl.ds(a * N, N), :].astype(BF16)
        pltpu.make_async_copy(obuf.at[ci], out.at[ci], out_sem).start()
        return carry

    lax.fori_loop(0, N, finish, 0)

    for cp in started:
        cp.wait_send()
    pltpu.make_async_copy(
        tsend.at[pl.ds(0, N * N - 1)], trecv.at[pl.ds(0, N * N - 1)], tsend_sem
    ).wait()
    pltpu.make_async_copy(obuf, out, out_sem).wait()


def shards(amplitudes, panels, fock_virt, occ_energy, strong_pairs):
    naux = panels.shape[2]
    hbm = pl.BlockSpec(memory_space=pl.ANY)
    vmem = pl.BlockSpec(memory_space=pltpu.VMEM)
    smem = pl.BlockSpec(memory_space=pltpu.SMEM)
    dma = pltpu.SemaphoreType.DMA
    result = pl.pallas_call(
        kernel,
        out_shape=jax.ShapeDtypeStruct((N, N, W * W), BF16),
        in_specs=[hbm, hbm, vmem, smem, smem],
        out_specs=hbm,
        scratch_shapes=[
            pltpu.VMEM((N, W, naux), BF16),
            pltpu.VMEM((N, W, naux), BF16),
            pltpu.VMEM((N, N, W * W), BF16),
            pltpu.VMEM((N * N, 32, 128), BF16),
            pltpu.VMEM((N * N, 32, 128), BF16),
            pltpu.VMEM((8, N * W, 128), F32),
            pltpu.VMEM((N, 32 * N, 128), F32),
            pltpu.VMEM((N, N, W * W), BF16),
            pltpu.VMEM((256, 256), BF16),
            dma((2,)),
            dma,
            dma,
            dma,
            dma,
            dma,
            dma((16,)),
            dma((N,)),
            dma((32,)),
            dma((N, 2)),
            pltpu.SemaphoreType.REGULAR,
        ],
        compiler_params=pltpu.CompilerParams(
            collective_id=0, has_side_effects=True, vmem_limit_bytes=52 * 2**20
        ),
        name="residual",
    )(
        amplitudes.reshape(N, N, W * W),
        panels,
        fock_virt,
        occ_energy,
        strong_pairs.reshape(N, N),
    )
    return result.reshape(amplitudes.shape)


def solution(mesh):
    placed = (
        P("row", None, None, None, "col", None, None),
        P(("row", "col"), None, None),
        P(),
        P(),
        P("row", None, None, None, "col", None),
    )
    return jax.shard_map(
        shards,
        mesh=mesh,
        in_specs=placed,
        out_specs=P("row", None, None, None, "col", None, None),
        check_vma=False,
    )
```

```python
import jax
import jax.numpy as jnp
from jax import lax
from jax.experimental import pallas as pl
from jax.experimental.pallas import tpu as pltpu
from jax.sharding import PartitionSpec as P

MESH = pl.DeviceIdType.MESH
F32 = jnp.float32
BF16 = jnp.bfloat16
N = 16
W = 64
NT = (((1,), (1,)), ((), ()))
PLAN = (
    "Z0", "Z1", "Y", "L", "X", "in", "prep", "ready", "y00", "z0", "z1", "zl", "T02", "f0",
    "T24", "f1", "T46", "y10", "T68", "y30", "x1", "x2", "x3", "x4", "y20",
)
CHUNKS = 2


def kernel(
    amp, panel, fock_in, occ_in, flags_in, out,
    left, right, tin, tsend, trecv, big, flat, obuf, diag, fock, occ, flags,
    psem, tsem, small_sem, tsend_sem, trecv_sem, own_sem, out_sem,
    lsend, lrecv, rsend, rrecv, ready,
):
    r = lax.axis_index("row")
    c = lax.axis_index("col")
    y, zh = r // 4, r % 4
    x, low = c // 4, c % 4

    def rows(dy, dz):
        return (y + dy + 4) % 4 * 4 + (zh + dz + 4) % 4

    def cols(dx):
        return (x + dx + 4) % 4 * 4 + low

    sib = c + 1 - 2 * (c % 2)
    zl_c = c + 2 - 4 * (low // 2)

    load_left = pltpu.make_async_copy(panel.at[0], left.at[c], psem.at[0])
    load_right = pltpu.make_async_copy(panel.at[0], right.at[r], psem.at[1])
    load_t = pltpu.make_async_copy(amp, tin, tsem)
    load_left.start()
    load_right.start()
    load_t.start()
    small = [
        pltpu.make_async_copy(src, dst, small_sem.at[i])
        for i, (src, dst) in enumerate(((fock_in, fock), (occ_in, occ), (flags_in, flags)))
    ]
    for cp in small:
        cp.start()

    bar = pltpu.get_barrier_semaphore()

    def greet(i, carry):
        pl.semaphore_signal(bar, inc=1, device_id=(r, (c + i) % N), device_id_type=MESH)
        pl.semaphore_signal(bar, inc=1, device_id=((r + i) % N, c), device_id_type=MESH)
        return carry

    lax.fori_loop(1, N, greet, 0)

    pl.semaphore_wait(bar, 2 * (N - 1))

    started = []

    def send_left(slot, col, k):
        cp = pltpu.make_async_remote_copy(
            src_ref=left.at[slot], dst_ref=left.at[slot],
            send_sem=lsend.at[k], recv_sem=lrecv.at[slot],
            device_id=(r, col), device_id_type=MESH,
        )
        cp.start()
        started.append(cp)

    def got_left(slot):
        pltpu.make_async_remote_copy(
            src_ref=left.at[slot], dst_ref=left.at[slot],
            send_sem=lsend.at[0], recv_sem=lrecv.at[slot],
            device_id=(r, sib), device_id_type=MESH,
        ).wait_recv()

    def half(slot, h):
        return right.at[slot, pl.ds(h * (W // CHUNKS), W // CHUNKS)]

    def send_right(slot, h, row, k):
        cp = pltpu.make_async_remote_copy(
            src_ref=half(slot, h), dst_ref=half(slot, h),
            send_sem=rsend.at[k], recv_sem=rrecv.at[slot, h],
            device_id=(row, c), device_id_type=MESH,
        )
        cp.start()
        started.append(cp)

    def got_right(slot, h):
        pltpu.make_async_remote_copy(
            src_ref=half(slot, h), dst_ref=half(slot, h),
            send_sem=rsend.at[0], recv_sem=rrecv.at[slot, h],
            device_id=(rows(1, 0), c), device_id_type=MESH,
        ).wait_recv()

    up_z, down_z, far_z = rows(0, 1), rows(0, -1), rows(0, 2)
    up_y, down_y = rows(1, 0), rows(-1, 0)
    next_left, next_right = iter(range(16)), iter(range(64))

    def push_left(slot, cols_to):
        for col in cols_to:
            send_left(slot, col, next(next_left))

    def push_right(slot, h, rows_to):
        for row in rows_to:
            send_right(slot, h, row, next(next_right))

    def all_in():
        def tell(i, carry):
            pl.semaphore_signal(
                ready, inc=1, device_id=((r + i) % N, c), device_id_type=MESH
            )
            return carry

        lax.fori_loop(1, N, tell, 0)

    low_lanes = lax.broadcasted_iota(jnp.int32, (32, 128), 1) < W

    def pair_up(first, second):
        return (
            jnp.where(low_lanes, first, pltpu.roll(second, W, 1)),
            jnp.where(low_lanes, pltpu.roll(first, W, 1), second),
        )

    def spread_amp(step, carry):
        p = (c // 2 + step) % 8
        for f in range(2):
            ci = 2 * p + f
            for a in range(32):
                flat[ci, pl.ds(a * N, N), :] = tin[ci, :, pl.ds(a * 128, 128)].astype(F32)
            for q in range(8):
                even, odd = pair_up(
                    flat[ci, pl.ds(2 * q, 32, stride=N), :],
                    flat[ci, pl.ds(2 * q + 1, 32, stride=N), :],
                )
                big[q, pl.ds(ci * W, 32, stride=2), :] = even
                big[q, pl.ds(ci * W + 1, 32, stride=2), :] = odd
        for q in range(8):
            block = big[q, pl.ds(pl.multiple_of(p * 128, 128), 128), :].T
            for g in range(2):
                first, second = pair_up(
                    block[g * W : g * W + 32], block[g * W + 32 : g * W + W]
                )
                tsend[2 * p * N + 2 * q + g] = first.astype(BF16)
                tsend[(2 * p + 1) * N + 2 * q + g] = second.astype(BF16)
        return carry

    def prepare():
        load_t.wait()
        lax.fori_loop(0, 8, spread_amp, 0)
        own_tile.start()

    own_tile = pltpu.make_async_copy(
        tsend.at[c * N + r], trecv.at[c * N + r], own_sem
    )

    def send_tiles(first, last):
        def route(k, carry):
            ci = (c // 2 * 2 + k // N) % N
            rj = (r + k) % N

            @pl.when(jnp.logical_or(rj != r, ci != c))
            def _():
                pltpu.make_async_remote_copy(
                    src_ref=tsend.at[ci * N + rj], dst_ref=trecv.at[c * N + r],
                    send_sem=tsend_sem, recv_sem=trecv_sem,
                    device_id=(rj, ci), device_id_type=MESH,
                ).start()

            return carry

        lax.fori_loop(first * 32, last * 32, route, 0)

    def own_z(h):
        if h == 0:
            load_right.wait()
        push_right(r, h, (down_z, up_z))

    def own_y():
        for h in range(CHUNKS):
            push_right(r, h, (up_y, down_y))

    def own_l():
        load_left.wait()
        push_left(c, (zl_c, sib))

    def own_x():
        push_left(c, (cols(1), cols(-1), cols(2)))

    def pass_zl():
        got_left(zl_c)
        push_left(zl_c, (sib, cols(1), cols(-1), cols(2)))

    def pass_z(h):
        for slot, on, mine in ((up_z, down_z, 0), (down_z, up_z, 1)):
            got_right(slot, h)
            passed = (on,) if h * 2 // CHUNKS == mine else ()
            push_right(slot, h, passed + (up_y, down_y))

    def pass_z2(h):
        got_right(far_z, h)
        push_right(far_z, h, (up_y, down_y))

    def pass_y(dz, h):
        got_right(rows(-1, dz), h)
        push_right(rows(-1, dz), h, (up_y,))
        got_right(rows(1, dz), h + CHUNKS // 2)
        push_right(rows(1, dz), h + CHUNKS // 2, (down_y,))

    other_zl = 2 - 4 * (low // 2)

    def pass_x(dx, zl):
        slot = cols(dx) + zl * other_zl
        got_left(slot)
        push_left(slot, (sib,))

    steps = {
        "Y": own_y, "L": own_l, "X": own_x, "prep": prepare, "zl": pass_zl,
        "in": all_in, "ready": lambda: pl.semaphore_wait(ready, N - 1),
        "x1": lambda: (pass_x(1, 0), pass_x(-1, 0)), "x2": lambda: pass_x(2, 0),
        "x3": lambda: (pass_x(1, 1), pass_x(-1, 1)), "x4": lambda: pass_x(2, 1),
    }
    numbered = {"Z": own_z, "z": pass_z, "f": pass_z2, "y": pass_y, "T": send_tiles}
    for name in PLAN:
        if name in steps:
            steps[name]()
        else:
            numbered[name[0]](*(int(digit) for digit in name[1:]))

    for cp in small:
        cp.wait()

    spread = (
        lax.broadcasted_iota(jnp.int32, (256, W), 0) % W
        == lax.broadcasted_iota(jnp.int32, (256, W), 1)
    ).astype(BF16)
    wide = jnp.dot(spread, fock[...], preferred_element_type=F32).astype(BF16)
    wide = lax.dot_general(wide, spread, NT, preferred_element_type=F32)
    same = (
        lax.broadcasted_iota(jnp.int32, (256, 256), 0) // W
        == lax.broadcasted_iota(jnp.int32, (256, 256), 1) // W
    )
    diag[...] = jnp.where(same, wide, 0.0).astype(BF16)

    own_tile.wait()
    pltpu.make_async_copy(
        tsend.at[pl.ds(0, N * N - 1)], trecv.at[pl.ds(0, N * N - 1)], trecv_sem
    ).wait()

    def linear(step, carry):
        for f in range(4):
            ci = step * 4 + f
            for q in range(8):
                top, bottom = pair_up(
                    trecv[ci * N + 2 * q].astype(F32), trecv[ci * N + 2 * q + 1].astype(F32)
                )
                span = pl.ds(pl.multiple_of(ci * W, W), 32)
                big[q, span, :] = big[q, span, :] + top
                span = pl.ds(pl.multiple_of(ci * W + 32, 32), 32)
                big[q, span, :] = big[q, span, :] + bottom
        span = pl.ds(pl.multiple_of(step * 256, 256), 256)
        which = lax.broadcasted_iota(jnp.int32, (256, 256), 0) // W
        first_e = jnp.zeros((256, 256), F32)
        for f in range(4):
            first_e = jnp.where(which == f, occ[r * N + step * 4 + f], first_e)
        which = lax.broadcasted_iota(jnp.int32, (256, 256), 1) // W
        for g in range(4):
            s = jnp.concatenate([big[2 * g, span, :], big[2 * g + 1, span, :]], axis=1)
            energy = first_e
            for f in range(4):
                energy = energy + jnp.where(which == f, occ[(4 * g + f) * N + c], 0.0)
            sb = s.astype(BF16)
            total = jnp.dot(diag[...], sb, preferred_element_type=F32)
            total = total + lax.dot_general(sb, diag[...], NT, preferred_element_type=F32)
            total = total - energy * s
            big[2 * g, span, :] = total[:, :128]
            big[2 * g + 1, span, :] = total[:, 128:]
        return carry

    lax.fori_loop(0, 4, linear, 0)

    for xs in range(4):
        for b in range(2):
            got_left(xs * 4 + b * 2 + 1 - c % 2)

    def group(dy):
        g = (y + dy + 4) % 4
        block = right.at[pl.ds(pl.multiple_of(g * 4, 4), 4)]

        def part(step, carry):
            span = pl.ds(pl.multiple_of(step * 256, 256), 256)
            lhs = left[pl.ds(step * 4, 4)].reshape(256, 4096)
            rhs = block[...].reshape(256, 4096)
            exch = lax.dot_general(lhs, rhs, NT, preferred_element_type=F32)
            for q in range(2):
                big[2 * g + q, span, :] = (
                    big[2 * g + q, span, :] + 2.0 * exch[:, q * 128 : q * 128 + 128]
                )
            for f in range(4):
                ci = step * 4 + f
                for q in range(2):
                    rj = 4 * g + 2 * q
                    even = big[2 * g + q, pl.ds(ci * W, 32, stride=2), :]
                    odd = big[2 * g + q, pl.ds(ci * W + 1, 32, stride=2), :]
                    one, two = pair_up(even, odd)
                    flat[ci, pl.ds(rj, 32, stride=N), :] = one * flags[ci, rj].astype(F32)
                    flat[ci, pl.ds(rj + 1, 32, stride=N), :] = (
                        two * flags[ci, rj + 1].astype(F32)
                    )
            return carry

        lax.fori_loop(0, 4, part, 0)

    group(0)
    for dy, missing in ((1, (0, 1)), (-1, (1, 2)), (2, (0, 2))):
        for h in range(missing[0] * CHUNKS // 2, missing[1] * CHUNKS // 2):
            for dz in (0, 1, -1, 2):
                got_right(rows(dy, dz), h)
        group(dy)

    def finish(ci, carry):
        for a in range(32):
            obuf[ci, :, pl.ds(a * 128, 128)] = flat[ci, pl.ds(a * N, N), :].astype(BF16)
        pltpu.make_async_copy(obuf.at[ci], out.at[ci], out_sem).start()
        return carry

    lax.fori_loop(0, N, finish, 0)

    for cp in started:
        cp.wait_send()
    pltpu.make_async_copy(
        tsend.at[pl.ds(0, N * N - 1)], trecv.at[pl.ds(0, N * N - 1)], tsend_sem
    ).wait()
    pltpu.make_async_copy(obuf, out, out_sem).wait()


def shards(amplitudes, panels, fock_virt, occ_energy, strong_pairs):
    naux = panels.shape[2]
    hbm = pl.BlockSpec(memory_space=pl.ANY)
    dma = pltpu.SemaphoreType.DMA
    result = pl.pallas_call(
        kernel,
        out_shape=jax.ShapeDtypeStruct((N, N, W * W), BF16),
        in_specs=[hbm] * 5,
        out_specs=hbm,
        scratch_shapes=[
            pltpu.VMEM((N, W, naux), BF16),
            pltpu.VMEM((N, W, naux), BF16),
            pltpu.VMEM((N, N, W * W), BF16),
            pltpu.VMEM((N * N, 32, 128), BF16),
            pltpu.VMEM((N * N, 32, 128), BF16),
            pltpu.VMEM((8, N * W, 128), F32),
            pltpu.VMEM((N, 32 * N, 128), F32),
            pltpu.VMEM((N, N, W * W), BF16),
            pltpu.VMEM((256, 256), BF16),
            pltpu.VMEM((W, W), BF16),
            pltpu.SMEM((N * N,), F32),
            pltpu.SMEM((N, N), jnp.int32),
            dma((2,)),
            dma,
            dma((3,)),
            dma,
            dma,
            dma,
            dma,
            dma((16,)),
            dma((N,)),
            dma((64,)),
            dma((N, CHUNKS)),
            pltpu.SemaphoreType.REGULAR,
        ],
        compiler_params=pltpu.CompilerParams(
            collective_id=0, has_side_effects=True, vmem_limit_bytes=60 * 2**20
        ),
        name="residual",
    )(
        amplitudes.reshape(N, N, W * W),
        panels,
        fock_virt,
        occ_energy,
        strong_pairs.reshape(N, N),
    )
    return result.reshape(amplitudes.shape)


def solution(mesh):
    placed = (
        P("row", None, None, None, "col", None, None),
        P(("row", "col"), None, None),
        P(),
        P(),
        P("row", None, None, None, "col", None),
    )
    return jax.shard_map(
        shards,
        mesh=mesh,
        in_specs=placed,
        out_specs=P("row", None, None, None, "col", None, None),
        check_vma=False,
    )
```

```python
import jax
import jax.numpy as jnp
from jax import lax
from jax.experimental import pallas as pl
from jax.experimental.pallas import tpu as pltpu
from jax.sharding import PartitionSpec as P

MESH = pl.DeviceIdType.MESH
F32 = jnp.float32
BF16 = jnp.bfloat16
N = 16
W = 64
NT = (((1,), (1,)), ((), ()))
PLAN = (
    "Z0", "Z1", "Y", "L", "X", "g0", "p04", "g1", "p48", "g2", "y00", "g3", "z0", "g4", "z1",
    "g5", "zl", "ready", "T02", "f0", "T24", "f1", "T46", "y10", "T68", "y30", "x1", "x2", "x3",
    "x4", "y20", "left", "m0", "m1", "m3", "lin", "s0", "s1", "s3", "e2",
)
CHUNKS = 2


def kernel(
    amp, panel, fock_in, occ_in, flags_in, obuf,
    left, right, tin, tsend, trecv, big, acc, flat, diag, fock, occ, flags,
    psem, tsem, small_sem, tsend_sem, trecv_sem, own_sem,
    lsend, lrecv, rsend, rrecv, ready,
):
    r = lax.axis_index("row")
    c = lax.axis_index("col")
    y, zh = r // 4, r % 4
    x, low = c // 4, c % 4

    def rows(dy, dz):
        return (y + dy + 4) % 4 * 4 + (zh + dz + 4) % 4

    def cols(dx):
        return (x + dx + 4) % 4 * 4 + low

    sib = c + 1 - 2 * (c % 2)
    zl_c = c + 2 - 4 * (low // 2)

    load_left = pltpu.make_async_copy(panel.at[0], left.at[c], psem.at[0])
    load_right = pltpu.make_async_copy(panel.at[0], right.at[zh * 4 + y], psem.at[1])
    load_t = pltpu.make_async_copy(amp, tin, tsem)
    load_left.start()
    load_right.start()
    load_t.start()
    small = [
        pltpu.make_async_copy(src, dst, small_sem.at[i])
        for i, (src, dst) in enumerate(((fock_in, fock), (occ_in, occ), (flags_in, flags)))
    ]
    for cp in small:
        cp.start()

    bar = pltpu.get_barrier_semaphore()

    partners = [(r, col) for col in (sib, zl_c, cols(1), cols(-1), cols(2))]
    partners += [(row, c) for row in (rows(0, 1), rows(0, -1), rows(1, 0), rows(-1, 0))]
    for partner in partners:
        pl.semaphore_signal(bar, inc=1, device_id=partner, device_id_type=MESH)
    pl.semaphore_wait(bar, len(partners))

    started = []

    def send_left(slot, col, k):
        cp = pltpu.make_async_remote_copy(
            src_ref=left.at[slot], dst_ref=left.at[slot],
            send_sem=lsend.at[k], recv_sem=lrecv.at[slot],
            device_id=(r, col), device_id_type=MESH,
        )
        cp.start()
        started.append(cp)

    def got_left(slot):
        pltpu.make_async_remote_copy(
            src_ref=left.at[slot], dst_ref=left.at[slot],
            send_sem=lsend.at[0], recv_sem=lrecv.at[slot],
            device_id=(r, sib), device_id_type=MESH,
        ).wait_recv()

    def half(slot, h):
        return right.at[slot % 4 * 4 + slot // 4, pl.ds(h * (W // CHUNKS), W // CHUNKS)]

    def send_right(slot, h, row, k):
        cp = pltpu.make_async_remote_copy(
            src_ref=half(slot, h), dst_ref=half(slot, h),
            send_sem=rsend.at[k], recv_sem=rrecv.at[slot, h],
            device_id=(row, c), device_id_type=MESH,
        )
        cp.start()
        started.append(cp)

    def got_right(slot, h):
        pltpu.make_async_remote_copy(
            src_ref=half(slot, h), dst_ref=half(slot, h),
            send_sem=rsend.at[0], recv_sem=rrecv.at[slot, h],
            device_id=(rows(1, 0), c), device_id_type=MESH,
        ).wait_recv()

    up_z, down_z, far_z = rows(0, 1), rows(0, -1), rows(0, 2)
    up_y, down_y = rows(1, 0), rows(-1, 0)
    next_left, next_right = iter(range(16)), iter(range(64))

    def push_left(slot, cols_to):
        for col in cols_to:
            send_left(slot, col, next(next_left))

    def push_right(slot, h, rows_to):
        for row in rows_to:
            send_right(slot, h, row, next(next_right))

    rounds = (
        (partners[0],), (partners[1],), partners[5:7], partners[5:7], partners[7:], partners[7:],
    )

    def hear(i):
        pl.semaphore_wait(ready.at[i], len(rounds[i]))

    def tell(i):
        if i:
            hear(i - 1)
        for partner in rounds[i]:
            pl.semaphore_signal(
                ready.at[i], inc=1, device_id=partner, device_id_type=MESH
            )

    low_lanes = lax.broadcasted_iota(jnp.int32, (32, 128), 1) < W

    def pair_up(first, second):
        return (
            jnp.where(low_lanes, first, pltpu.roll(second, W, 1)),
            jnp.where(low_lanes, pltpu.roll(first, W, 1), second),
        )

    def at(place):
        return place % 4 * 4 + place // 4

    def spread_amp(step, carry):
        p = (c // 2 + step) % 8
        for f in range(2):
            ci = 2 * p + f
            for a in range(32):
                flat[ci, pl.ds(a * N, N), :] = tin[ci, :, pl.ds(a * 128, 128)].astype(F32)
            for q in range(8):
                even, odd = pair_up(
                    flat[ci, pl.ds(at(2 * q), 32, stride=N), :],
                    flat[ci, pl.ds(at(2 * q + 1), 32, stride=N), :],
                )
                big[q, pl.ds(ci * W, 32, stride=2), :] = even
                big[q, pl.ds(ci * W + 1, 32, stride=2), :] = odd
        for q in range(8):
            block = big[q, pl.ds(pl.multiple_of(p * 128, 128), 128), :].T
            for g in range(2):
                first, second = pair_up(
                    block[g * W : g * W + 32], block[g * W + 32 : g * W + W]
                )
                tsend[2 * p * N + at(2 * q + g)] = first.astype(BF16)
                tsend[(2 * p + 1) * N + at(2 * q + g)] = second.astype(BF16)
        return carry

    def prepare(first, last):
        if first == 0:
            load_t.wait()
        lax.fori_loop(first, last, spread_amp, 0)
        if last == 8:
            own_tile.start()

    own_tile = pltpu.make_async_copy(
        tsend.at[c * N + r], trecv.at[c * N + r], own_sem
    )

    def send_tiles(first, last):
        def route(k, carry):
            ci = (c + k // N) % N
            rj = (r + k) % N
            pltpu.make_async_remote_copy(
                src_ref=tsend.at[ci * N + rj], dst_ref=trecv.at[c * N + r],
                send_sem=tsend_sem, recv_sem=trecv_sem,
                device_id=(rj, ci), device_id_type=MESH,
            ).start()
            return carry

        lax.fori_loop(max(first * 32, 1), last * 32, route, 0)

    def own_z(h):
        if h == 0:
            load_right.wait()
        push_right(r, h, (down_z, up_z))

    def own_y():
        for h in range(CHUNKS):
            push_right(r, h, (up_y, down_y))

    def own_l():
        load_left.wait()
        push_left(c, (zl_c, sib))

    def own_x():
        push_left(c, (cols(1), cols(-1), cols(2)))

    def pass_zl():
        got_left(zl_c)
        push_left(zl_c, (sib, cols(1), cols(-1), cols(2)))

    def pass_z(h):
        for slot, on, mine in ((up_z, down_z, 0), (down_z, up_z, 1)):
            got_right(slot, h)
            passed = (on,) if h * 2 // CHUNKS == mine else ()
            push_right(slot, h, passed + (up_y, down_y))

    def pass_z2(h):
        got_right(far_z, h)
        push_right(far_z, h, (up_y, down_y))

    def pass_y(dz, h):
        got_right(rows(-1, dz), h)
        push_right(rows(-1, dz), h, (up_y,))
        got_right(rows(1, dz), h + CHUNKS // 2)
        push_right(rows(1, dz), h + CHUNKS // 2, (down_y,))

    other_zl = 2 - 4 * (low // 2)

    def pass_x(dx, zl):
        slot = cols(dx) + zl * other_zl
        got_left(slot)
        push_left(slot, (sib,))

    def linear(step, carry):
        for f in range(4):
            ci = step * 4 + f
            for q in range(8):
                top, bottom = pair_up(
                    trecv[ci * N + at(2 * q)].astype(F32),
                    trecv[ci * N + at(2 * q + 1)].astype(F32),
                )
                span = pl.ds(pl.multiple_of(ci * W, W), 32)
                big[q, span, :] = big[q, span, :] + top
                span = pl.ds(pl.multiple_of(ci * W + 32, 32), 32)
                big[q, span, :] = big[q, span, :] + bottom
        span = pl.ds(pl.multiple_of(step * 256, 256), 256)
        which = lax.broadcasted_iota(jnp.int32, (256, 256), 0) // W
        first_e = jnp.zeros((256, 256), F32)
        for f in range(4):
            first_e = jnp.where(which == f, occ[r * N + step * 4 + f], first_e)
        which = lax.broadcasted_iota(jnp.int32, (256, 256), 1) // W
        for g in range(4):
            s = jnp.concatenate([big[2 * g, span, :], big[2 * g + 1, span, :]], axis=1)
            energy = first_e
            for f in range(4):
                energy = energy + jnp.where(which == f, occ[at(4 * g + f) * N + c], 0.0)
            sb = s.astype(BF16)
            total = jnp.dot(diag[...], sb, preferred_element_type=F32)
            total = total + lax.dot_general(sb, diag[...], NT, preferred_element_type=F32)
            total = total - energy * s
            big[2 * g, span, :] = total[:, :128]
            big[2 * g + 1, span, :] = total[:, 128:]
        return carry

    def mirrors():
        own_tile.wait()
        pltpu.make_async_copy(
            tsend.at[pl.ds(0, N * N - 1)], trecv.at[pl.ds(0, N * N - 1)], trecv_sem
        ).wait()
        lax.fori_loop(0, 4, linear, 0)

    def all_left():
        for xs in range(4):
            for b in range(2):
                got_left(xs * 4 + b * 2 + 1 - c % 2)

    def multiply(step, g):
        lhs = left[pl.ds(step * 8, 8)].reshape(512, 4096)
        rhs = right[pl.ds(pl.multiple_of(g * 4, 4), 4)].reshape(256, 4096)
        exch = lax.dot_general(lhs, rhs, NT, preferred_element_type=F32)
        return 2.0 * exch[:, :128], 2.0 * exch[:, 128:]

    def place(step, g):
        for f in range(8):
            ci = step * 8 + f
            for q in range(2):
                pair = pair_up(
                    big[2 * g + q, pl.ds(ci * W, 32, stride=2), :],
                    big[2 * g + q, pl.ds(ci * W + 1, 32, stride=2), :],
                )
                for tile, ys in zip(pair, (2 * q, 2 * q + 1)):
                    rj = ys * 4 + g
                    flat[ci, pl.ds(rj, 32, stride=N), :] = tile * flags[ci, rj].astype(F32)

    def arrived(dz):
        for h in range(CHUNKS):
            got_right(rows(1 if h < CHUNKS // 2 else -1, dz), h)
            got_right(rows(2, dz), h)

    def exchange(dz):
        g = (zh + dz + 4) % 4
        arrived(dz)

        def part(step, carry):
            span = pl.ds(pl.multiple_of(step * 512, 512), 512)
            acc[2 * g, span, :], acc[2 * g + 1, span, :] = multiply(step, g)
            return carry

        lax.fori_loop(0, 2, part, 0)

    def settle(dz):
        g = (zh + dz + 4) % 4

        def part(step, carry):
            span = pl.ds(pl.multiple_of(step * 512, 512), 512)
            for q in range(2):
                big[2 * g + q, span, :] = big[2 * g + q, span, :] + acc[2 * g + q, span, :]
            place(step, g)
            return carry

        lax.fori_loop(0, 2, part, 0)

    def last(dz):
        g = (zh + dz + 4) % 4
        arrived(dz)

        def part(step, carry):
            span = pl.ds(pl.multiple_of(step * 512, 512), 512)
            for q, x in enumerate(multiply(step, g)):
                big[2 * g + q, span, :] = big[2 * g + q, span, :] + x
            place(step, g)
            for f in range(8):
                ci = step * 8 + f
                for a in range(32):
                    obuf[ci, :, pl.ds(a * 128, 128)] = flat[ci, pl.ds(a * N, N), :].astype(BF16)
            return carry

        lax.fori_loop(0, 2, part, 0)

    for cp in small:
        cp.wait()

    spread = (
        lax.broadcasted_iota(jnp.int32, (256, W), 0) % W
        == lax.broadcasted_iota(jnp.int32, (256, W), 1)
    ).astype(BF16)
    wide = jnp.dot(spread, fock[...], preferred_element_type=F32).astype(BF16)
    wide = lax.dot_general(wide, spread, NT, preferred_element_type=F32)
    same = (
        lax.broadcasted_iota(jnp.int32, (256, 256), 0) // W
        == lax.broadcasted_iota(jnp.int32, (256, 256), 1) // W
    )
    diag[...] = jnp.where(same, wide, 0.0).astype(BF16)

    steps = {
        "Y": own_y, "L": own_l, "X": own_x, "zl": pass_zl, "ready": lambda: hear(5),
        "x1": lambda: (pass_x(1, 0), pass_x(-1, 0)), "x2": lambda: pass_x(2, 0),
        "x3": lambda: (pass_x(1, 1), pass_x(-1, 1)), "x4": lambda: pass_x(2, 1),
        "left": all_left, "lin": mirrors,
    }
    numbered = {
        "Z": own_z, "z": pass_z, "f": pass_z2, "y": pass_y, "T": send_tiles,
        "p": prepare, "g": tell,
        "m": exchange, "s": settle, "e": last,
    }
    for name in PLAN:
        if name in steps:
            steps[name]()
        else:
            numbered[name[0]](*(int(digit) for digit in name[1:]))

    for cp in started:
        cp.wait_send()
    pltpu.make_async_copy(
        tsend.at[pl.ds(0, N * N - 1)], trecv.at[pl.ds(0, N * N - 1)], tsend_sem
    ).wait()


def put_out(held, out, sem):
    copies = [pltpu.make_async_copy(held.at[i], out.at[i], sem.at[i]) for i in range(N)]
    for copy in copies:
        copy.start()
    for copy in copies:
        copy.wait()


def shards(amplitudes, panels, fock_virt, occ_energy, strong_pairs):
    naux = panels.shape[2]
    hbm = pl.BlockSpec(memory_space=pltpu.HBM)
    vmem = pl.BlockSpec(memory_space=pltpu.VMEM)
    dma = pltpu.SemaphoreType.DMA
    result = pl.pallas_call(
        kernel,
        out_shape=pltpu.VMEM((N, N, W * W), BF16),
        in_specs=[hbm] * 5,
        out_specs=vmem,
        scratch_shapes=[
            pltpu.VMEM((N, W, naux), BF16),
            pltpu.VMEM((N, W, naux), BF16),
            pltpu.VMEM((N, N, W * W), BF16),
            pltpu.VMEM((N * N, 32, 128), BF16),
            pltpu.VMEM((N * N, 32, 128), BF16),
            pltpu.VMEM((8, N * W, 128), F32),
            pltpu.VMEM((8, N * W, 128), F32),
            pltpu.VMEM((N, 32 * N, 128), F32),
            pltpu.VMEM((256, 256), BF16),
            pltpu.VMEM((W, W), BF16),
            pltpu.SMEM((N * N,), F32),
            pltpu.SMEM((N, N), jnp.int32),
            dma((2,)),
            dma,
            dma((3,)),
            dma,
            dma,
            dma,
            dma((16,)),
            dma((N,)),
            dma((64,)),
            dma((N, CHUNKS)),
            pltpu.SemaphoreType.REGULAR((6,)),
        ],
        compiler_params=pltpu.CompilerParams(
            collective_id=0, has_side_effects=True, vmem_limit_bytes=56 * 2**20
        ),
        name="residual",
    )(
        amplitudes.reshape(N, N, W * W),
        panels,
        fock_virt,
        occ_energy,
        strong_pairs.reshape(N, N),
    )
    result = pl.pallas_call(
        put_out,
        out_shape=jax.ShapeDtypeStruct((N, N, W * W), BF16),
        in_specs=[pl.BlockSpec(memory_space=pltpu.VMEM)],
        out_specs=pl.BlockSpec(memory_space=pl.ANY),
        scratch_shapes=[dma((N,))],
        name="put_out",
    )(result)
    return result.reshape(amplitudes.shape)


def solution(mesh):
    placed = (
        P("row", None, None, None, "col", None, None),
        P(("row", "col"), None, None),
        P(),
        P(),
        P("row", None, None, None, "col", None),
    )
    return jax.shard_map(
        shards,
        mesh=mesh,
        in_specs=placed,
        out_specs=P("row", None, None, None, "col", None, None),
        check_vma=False,
    )
```

```python
import jax
import jax.numpy as jnp
from jax import lax
from jax.experimental import pallas as pl
from jax.experimental.pallas import tpu as pltpu
from jax.sharding import PartitionSpec as P

MESH = pl.DeviceIdType.MESH
F32 = jnp.float32
BF16 = jnp.bfloat16
N = 16
W = 64
NT = (((1,), (1,)), ((), ()))
PLAN = (
    "Z0", "Z1", "Y", "S", "L", "X", "g0", "p04", "g1", "p48", "g2", "y00", "g3", "z0", "g4",
    "z1", "g5", "zl", "ready", "T02", "f0", "T24", "f1", "T46", "y10", "T68", "y30", "x1",
    "x2", "x3", "x4", "y20", "left", "m0", "m1", "m3", "lin", "s0", "s1", "s3", "e2",
)
CHUNKS = 2


def kernel(
    amp, panel, fock_in, occ_in, flags_in, obuf,
    left, right, tin, tsend, trecv, big, acc, flat, diag, fock, occ, flags,
    psem, tsem, small_sem, tsend_sem, trecv_sem, own_sem,
    lsend, lrecv, rsend, rrecv, ready,
):
    r = lax.axis_index("row")
    c = lax.axis_index("col")
    y, zh = r // 4, r % 4
    x, low = c // 4, c % 4

    def rows(dy, dz):
        return (y + dy + 4) % 4 * 4 + (zh + dz + 4) % 4

    def cols(dx):
        return (x + dx + 4) % 4 * 4 + low

    sib = c + 1 - 2 * (c % 2)
    zl_c = c + 2 - 4 * (low // 2)

    load_left = pltpu.make_async_copy(panel.at[0], left.at[c], psem.at[0])
    load_right = pltpu.make_async_copy(panel.at[0], right.at[zh * 4 + y], psem.at[1])
    load_t = pltpu.make_async_copy(amp, tin, tsem)
    load_left.start()
    load_right.start()
    load_t.start()
    small = [
        pltpu.make_async_copy(src, dst, small_sem.at[i])
        for i, (src, dst) in enumerate(((fock_in, fock), (occ_in, occ), (flags_in, flags)))
    ]
    for cp in small:
        cp.start()

    bar = pltpu.get_barrier_semaphore()

    partners = [(r, col) for col in (sib, zl_c, cols(1), cols(-1), cols(2))]
    partners += [(row, c) for row in (rows(0, 1), rows(0, -1), rows(1, 0), rows(-1, 0))]
    for partner in partners:
        pl.semaphore_signal(bar, inc=1, device_id=partner, device_id_type=MESH)
    pl.semaphore_wait(bar, len(partners))

    started = []

    def send_left(slot, col, k):
        cp = pltpu.make_async_remote_copy(
            src_ref=left.at[slot], dst_ref=left.at[slot],
            send_sem=lsend.at[k], recv_sem=lrecv.at[slot],
            device_id=(r, col), device_id_type=MESH,
        )
        cp.start()
        started.append(cp)

    def got_left(slot):
        pltpu.make_async_remote_copy(
            src_ref=left.at[slot], dst_ref=left.at[slot],
            send_sem=lsend.at[0], recv_sem=lrecv.at[slot],
            device_id=(r, sib), device_id_type=MESH,
        ).wait_recv()

    def half(slot, h):
        return right.at[slot % 4 * 4 + slot // 4, pl.ds(h * (W // CHUNKS), W // CHUNKS)]

    def send_right(slot, h, row, k):
        cp = pltpu.make_async_remote_copy(
            src_ref=half(slot, h), dst_ref=half(slot, h),
            send_sem=rsend.at[k], recv_sem=rrecv.at[slot, h],
            device_id=(row, c), device_id_type=MESH,
        )
        cp.start()
        started.append(cp)

    def got_right(slot, h):
        pltpu.make_async_remote_copy(
            src_ref=half(slot, h), dst_ref=half(slot, h),
            send_sem=rsend.at[0], recv_sem=rrecv.at[slot, h],
            device_id=(rows(1, 0), c), device_id_type=MESH,
        ).wait_recv()

    up_z, down_z, far_z = rows(0, 1), rows(0, -1), rows(0, 2)
    up_y, down_y = rows(1, 0), rows(-1, 0)
    next_left, next_right = iter(range(16)), iter(range(64))

    def push_left(slot, cols_to):
        for col in cols_to:
            send_left(slot, col, next(next_left))

    def push_right(slot, h, rows_to):
        for row in rows_to:
            send_right(slot, h, row, next(next_right))

    rounds = (
        (partners[0],), (partners[1],), partners[5:7], partners[5:7], partners[7:], partners[7:],
    )

    def hear(i):
        pl.semaphore_wait(ready.at[i], len(rounds[i]))

    def tell(i):
        if i:
            hear(i - 1)
        for partner in rounds[i]:
            pl.semaphore_signal(
                ready.at[i], inc=1, device_id=partner, device_id_type=MESH
            )

    low_lanes = lax.broadcasted_iota(jnp.int32, (32, 128), 1) < W

    def pair_up(first, second):
        return (
            jnp.where(low_lanes, first, pltpu.roll(second, W, 1)),
            jnp.where(low_lanes, pltpu.roll(first, W, 1), second),
        )

    def at(place):
        return place % 4 * 4 + place // 4

    def spread_amp(step, carry):
        p = (c // 2 + step) % 8
        for f in range(2):
            ci = 2 * p + f
            for a in range(32):
                flat[ci, pl.ds(a * N, N), :] = tin[ci, :, pl.ds(a * 128, 128)].astype(F32)
            for q in range(8):
                even, odd = pair_up(
                    flat[ci, pl.ds(at(2 * q), 32, stride=N), :],
                    flat[ci, pl.ds(at(2 * q + 1), 32, stride=N), :],
                )
                big[q, pl.ds(ci * W, 32, stride=2), :] = even
                big[q, pl.ds(ci * W + 1, 32, stride=2), :] = odd
        for q in range(8):
            block = big[q, pl.ds(pl.multiple_of(p * 128, 128), 128), :].T
            for g in range(2):
                first, second = pair_up(
                    block[g * W : g * W + 32], block[g * W + 32 : g * W + W]
                )
                tsend[2 * p * N + at(2 * q + g)] = first.astype(BF16)
                tsend[(2 * p + 1) * N + at(2 * q + g)] = second.astype(BF16)
        return carry

    def prepare(first, last):
        if first == 0:
            load_t.wait()
        lax.fori_loop(first, last, spread_amp, 0)
        if last == 8:
            own_tile.start()

    own_tile = pltpu.make_async_copy(
        tsend.at[c * N + r], trecv.at[c * N + r], own_sem
    )

    def send_tiles(first, last):
        def route(k, carry):
            ci = (c + k // N) % N
            rj = (r + k) % N
            pltpu.make_async_remote_copy(
                src_ref=tsend.at[ci * N + rj], dst_ref=trecv.at[c * N + r],
                send_sem=tsend_sem, recv_sem=trecv_sem,
                device_id=(rj, ci), device_id_type=MESH,
            ).start()
            return carry

        lax.fori_loop(max(first * 32, 1), last * 32, route, 0)

    def own_z(h):
        if h == 0:
            load_right.wait()
        push_right(r, h, (down_z,))
        push_right(r, CHUNKS - 1 - h, (up_z,))

    def own_y():
        for h in range(CHUNKS):
            push_right(r, h, (up_y,))
            push_right(r, CHUNKS - 1 - h, (down_y,))

    def own_l():
        push_left(c, (zl_c,))

    def own_sib():
        load_left.wait()
        push_left(c, (sib,))

    def own_x():
        push_left(c, (cols(1), cols(-1), cols(2)))

    def pass_zl():
        got_left(zl_c)
        push_left(zl_c, (sib, cols(1), cols(-1), cols(2)))

    def pass_z(h):
        for slot, on, part in ((up_z, down_z, h), (down_z, up_z, CHUNKS - 1 - h)):
            got_right(slot, part)
            passed = (on,) if h < CHUNKS // 2 else ()
            push_right(slot, part, passed + (up_y, down_y))

    def pass_z2(h):
        got_right(far_z, h)
        push_right(far_z, h, (up_y, down_y))

    def pass_y(dz, h):
        for slot, on, part in (
            (rows(-1, dz), up_y, h), (rows(1, dz), down_y, CHUNKS - 1 - h),
        ):
            got_right(slot, part)
            push_right(slot, part, (on,))

    other_zl = 2 - 4 * (low // 2)

    def pass_x(dx, zl):
        slot = cols(dx) + zl * other_zl
        got_left(slot)
        push_left(slot, (sib,))

    def linear(step, carry):
        for f in range(4):
            ci = step * 4 + f
            for q in range(8):
                top, bottom = pair_up(
                    trecv[ci * N + at(2 * q)].astype(F32),
                    trecv[ci * N + at(2 * q + 1)].astype(F32),
                )
                span = pl.ds(pl.multiple_of(ci * W, W), 32)
                big[q, span, :] = big[q, span, :] + top
                span = pl.ds(pl.multiple_of(ci * W + 32, 32), 32)
                big[q, span, :] = big[q, span, :] + bottom
        span = pl.ds(pl.multiple_of(step * 256, 256), 256)
        which = lax.broadcasted_iota(jnp.int32, (256, 256), 0) // W
        first_e = jnp.zeros((256, 256), F32)
        for f in range(4):
            first_e = jnp.where(which == f, occ[r * N + step * 4 + f], first_e)
        which = lax.broadcasted_iota(jnp.int32, (256, 256), 1) // W
        for g in range(4):
            s = jnp.concatenate([big[2 * g, span, :], big[2 * g + 1, span, :]], axis=1)
            energy = first_e
            for f in range(4):
                energy = energy + jnp.where(which == f, occ[at(4 * g + f) * N + c], 0.0)
            sb = s.astype(BF16)
            total = jnp.dot(diag[...], sb, preferred_element_type=F32)
            total = total + lax.dot_general(sb, diag[...], NT, preferred_element_type=F32)
            total = total - energy * s
            big[2 * g, span, :] = total[:, :128]
            big[2 * g + 1, span, :] = total[:, 128:]
        return carry

    def mirrors():
        own_tile.wait()
        pltpu.make_async_copy(
            tsend.at[pl.ds(0, N * N - 1)], trecv.at[pl.ds(0, N * N - 1)], trecv_sem
        ).wait()
        lax.fori_loop(0, 4, linear, 0)

    def all_left():
        for xs in range(4):
            for b in range(2):
                got_left(xs * 4 + b * 2 + 1 - c % 2)

    def multiply(step, g):
        lhs = left[pl.ds(step * 8, 8)].reshape(512, 4096)
        rhs = right[pl.ds(pl.multiple_of(g * 4, 4), 4)].reshape(256, 4096)
        exch = lax.dot_general(lhs, rhs, NT, preferred_element_type=F32)
        return 2.0 * exch[:, :128], 2.0 * exch[:, 128:]

    def place(step, g):
        for f in range(8):
            ci = step * 8 + f
            for q in range(2):
                pair = pair_up(
                    big[2 * g + q, pl.ds(ci * W, 32, stride=2), :],
                    big[2 * g + q, pl.ds(ci * W + 1, 32, stride=2), :],
                )
                for tile, ys in zip(pair, (2 * q, 2 * q + 1)):
                    rj = ys * 4 + g
                    flat[ci, pl.ds(rj, 32, stride=N), :] = tile * flags[ci, rj].astype(F32)

    def arrived(dz):
        for h in range(CHUNKS):
            got_right(rows(1 if h < CHUNKS // 2 else -1, dz), h)
            got_right(rows(2, dz), h)

    def exchange(dz):
        g = (zh + dz + 4) % 4
        arrived(dz)

        def part(step, carry):
            span = pl.ds(pl.multiple_of(step * 512, 512), 512)
            acc[2 * g, span, :], acc[2 * g + 1, span, :] = multiply(step, g)
            return carry

        lax.fori_loop(0, 2, part, 0)

    def settle(dz):
        g = (zh + dz + 4) % 4

        def part(step, carry):
            span = pl.ds(pl.multiple_of(step * 512, 512), 512)
            for q in range(2):
                big[2 * g + q, span, :] = big[2 * g + q, span, :] + acc[2 * g + q, span, :]
            place(step, g)
            return carry

        lax.fori_loop(0, 2, part, 0)

    def last(dz):
        g = (zh + dz + 4) % 4
        arrived(dz)

        def part(step, carry):
            span = pl.ds(pl.multiple_of(step * 512, 512), 512)
            for q, x in enumerate(multiply(step, g)):
                big[2 * g + q, span, :] = big[2 * g + q, span, :] + x
            place(step, g)
            for f in range(8):
                ci = step * 8 + f
                for a in range(32):
                    obuf[ci, :, pl.ds(a * 128, 128)] = flat[ci, pl.ds(a * N, N), :].astype(BF16)
            return carry

        lax.fori_loop(0, 2, part, 0)

    for cp in small:
        cp.wait()

    spread = (
        lax.broadcasted_iota(jnp.int32, (256, W), 0) % W
        == lax.broadcasted_iota(jnp.int32, (256, W), 1)
    ).astype(BF16)
    wide = jnp.dot(spread, fock[...], preferred_element_type=F32).astype(BF16)
    wide = lax.dot_general(wide, spread, NT, preferred_element_type=F32)
    same = (
        lax.broadcasted_iota(jnp.int32, (256, 256), 0) // W
        == lax.broadcasted_iota(jnp.int32, (256, 256), 1) // W
    )
    diag[...] = jnp.where(same, wide, 0.0).astype(BF16)

    steps = {
        "Y": own_y, "S": own_sib, "L": own_l, "X": own_x, "zl": pass_zl, "ready": lambda: hear(5),
        "x1": lambda: (pass_x(1, 0), pass_x(-1, 0)), "x2": lambda: pass_x(2, 0),
        "x3": lambda: (pass_x(1, 1), pass_x(-1, 1)), "x4": lambda: pass_x(2, 1),
        "left": all_left, "lin": mirrors,
    }
    numbered = {
        "Z": own_z, "z": pass_z, "f": pass_z2, "y": pass_y, "T": send_tiles,
        "p": prepare, "g": tell,
        "m": exchange, "s": settle, "e": last,
    }
    for name in PLAN:
        if name in steps:
            steps[name]()
        else:
            numbered[name[0]](*(int(digit) for digit in name[1:]))

    for cp in started:
        cp.wait_send()
    pltpu.make_async_copy(
        tsend.at[pl.ds(0, N * N - 1)], trecv.at[pl.ds(0, N * N - 1)], tsend_sem
    ).wait()


def put_out(held, out, sem):
    copies = [pltpu.make_async_copy(held.at[i], out.at[i], sem.at[i]) for i in range(N)]
    for copy in copies:
        copy.start()
    for copy in copies:
        copy.wait()


def shards(amplitudes, panels, fock_virt, occ_energy, strong_pairs):
    naux = panels.shape[2]
    hbm = pl.BlockSpec(memory_space=pltpu.HBM)
    vmem = pl.BlockSpec(memory_space=pltpu.VMEM)
    dma = pltpu.SemaphoreType.DMA
    result = pl.pallas_call(
        kernel,
        out_shape=pltpu.VMEM((N, N, W * W), BF16),
        in_specs=[hbm] * 5,
        out_specs=vmem,
        scratch_shapes=[
            pltpu.VMEM((N, W, naux), BF16),
            pltpu.VMEM((N, W, naux), BF16),
            pltpu.VMEM((N, N, W * W), BF16),
            pltpu.VMEM((N * N, 32, 128), BF16),
            pltpu.VMEM((N * N, 32, 128), BF16),
            pltpu.VMEM((8, N * W, 128), F32),
            pltpu.VMEM((8, N * W, 128), F32),
            pltpu.VMEM((N, 32 * N, 128), F32),
            pltpu.VMEM((256, 256), BF16),
            pltpu.VMEM((W, W), BF16),
            pltpu.SMEM((N * N,), F32),
            pltpu.SMEM((N, N), jnp.int32),
            dma((2,)),
            dma,
            dma((3,)),
            dma,
            dma,
            dma,
            dma((16,)),
            dma((N,)),
            dma((64,)),
            dma((N, CHUNKS)),
            pltpu.SemaphoreType.REGULAR((6,)),
        ],
        compiler_params=pltpu.CompilerParams(
            collective_id=0, has_side_effects=True, vmem_limit_bytes=56 * 2**20
        ),
        name="residual",
    )(
        amplitudes.reshape(N, N, W * W),
        panels,
        fock_virt,
        occ_energy,
        strong_pairs.reshape(N, N),
    )
    result = pl.pallas_call(
        put_out,
        out_shape=jax.ShapeDtypeStruct((N, N, W * W), BF16),
        in_specs=[pl.BlockSpec(memory_space=pltpu.VMEM)],
        out_specs=pl.BlockSpec(memory_space=pltpu.HBM),
        scratch_shapes=[dma((N,))],
        compiler_params=pltpu.CompilerParams(vmem_limit_bytes=2**20),
        name="put_out",
    )(result)
    return result.reshape(amplitudes.shape)


def solution(mesh):
    placed = (
        P("row", None, None, None, "col", None, None),
        P(("row", "col"), None, None),
        P(),
        P(),
        P("row", None, None, None, "col", None),
    )
    return jax.shard_map(
        shards,
        mesh=mesh,
        in_specs=placed,
        out_specs=P("row", None, None, None, "col", None, None),
        check_vma=False,
    )
```

```python
import jax
import jax.numpy as jnp
from jax import lax
from jax.experimental import pallas as pl
from jax.experimental.pallas import tpu as pltpu
from jax.sharding import PartitionSpec as P

MESH = pl.DeviceIdType.MESH
F32 = jnp.float32
BF16 = jnp.bfloat16
N = 16
W = 64
NT = (((1,), (1,)), ((), ()))
PLAN = (
    "Z0", "Z1", "Y", "S", "L", "X", "g0", "p04", "g1", "p48", "g2", "g3", "g4", "g5", "ready",
    "T00", "y00", "z0", "z1", "zl", "T01", "T10", "f0", "T11", "T30", "f1", "T31", "T20", "y10",
    "T21", "y30", "x1", "x2", "x3", "x4", "left", "m0", "y20", "m1", "m3", "lin", "s0", "s1",
    "s3", "e2",
)
CHUNKS = 2


def kernel(
    amp, panel, fock_in, occ_in, flags_in, obuf,
    left, right, tin, tsend, trecv, big, acc, flat, diag, fock, occ, flags,
    psem, tsem, small_sem, tsend_sem, trecv_sem, own_sem,
    lsend, lrecv, rsend, rrecv, ready,
):
    r = lax.axis_index("row")
    c = lax.axis_index("col")
    y, zh = r // 4, r % 4
    x, low = c // 4, c % 4

    def rows(dy, dz):
        return (y + dy + 4) % 4 * 4 + (zh + dz + 4) % 4

    def cols(dx):
        return (x + dx + 4) % 4 * 4 + low

    sib = c + 1 - 2 * (c % 2)
    zl_c = c + 2 - 4 * (low // 2)

    load_left = pltpu.make_async_copy(panel.at[0], left.at[c], psem.at[0])
    load_right = pltpu.make_async_copy(panel.at[0], right.at[zh * 4 + y], psem.at[1])
    load_t = pltpu.make_async_copy(amp, tin, tsem)
    load_left.start()
    load_right.start()
    load_t.start()
    small = [
        pltpu.make_async_copy(src, dst, small_sem.at[i])
        for i, (src, dst) in enumerate(((fock_in, fock), (occ_in, occ), (flags_in, flags)))
    ]
    for cp in small:
        cp.start()

    bar = pltpu.get_barrier_semaphore()

    partners = [(r, col) for col in (sib, zl_c, cols(1), cols(-1), cols(2))]
    partners += [(row, c) for row in (rows(0, 1), rows(0, -1), rows(1, 0), rows(-1, 0))]
    for partner in partners:
        pl.semaphore_signal(bar, inc=1, device_id=partner, device_id_type=MESH)
    pl.semaphore_wait(bar, len(partners))

    started = []

    def send_left(slot, col, k):
        cp = pltpu.make_async_remote_copy(
            src_ref=left.at[slot], dst_ref=left.at[slot],
            send_sem=lsend.at[k], recv_sem=lrecv.at[slot],
            device_id=(r, col), device_id_type=MESH,
        )
        cp.start()
        started.append(cp)

    def got_left(slot):
        pltpu.make_async_remote_copy(
            src_ref=left.at[slot], dst_ref=left.at[slot],
            send_sem=lsend.at[0], recv_sem=lrecv.at[slot],
            device_id=(r, sib), device_id_type=MESH,
        ).wait_recv()

    def half(slot, h):
        return right.at[slot % 4 * 4 + slot // 4, pl.ds(h * (W // CHUNKS), W // CHUNKS)]

    def send_right(slot, h, row, k):
        cp = pltpu.make_async_remote_copy(
            src_ref=half(slot, h), dst_ref=half(slot, h),
            send_sem=rsend.at[k], recv_sem=rrecv.at[slot, h],
            device_id=(row, c), device_id_type=MESH,
        )
        cp.start()
        started.append(cp)

    def got_right(slot, h):
        pltpu.make_async_remote_copy(
            src_ref=half(slot, h), dst_ref=half(slot, h),
            send_sem=rsend.at[0], recv_sem=rrecv.at[slot, h],
            device_id=(rows(1, 0), c), device_id_type=MESH,
        ).wait_recv()

    up_z, down_z, far_z = rows(0, 1), rows(0, -1), rows(0, 2)
    up_y, down_y = rows(1, 0), rows(-1, 0)
    next_left, next_right = iter(range(16)), iter(range(64))

    def push_left(slot, cols_to):
        for col in cols_to:
            send_left(slot, col, next(next_left))

    def push_right(slot, h, rows_to):
        for row in rows_to:
            send_right(slot, h, row, next(next_right))

    rounds = (
        (partners[0],), (partners[1],), partners[5:7], partners[5:7], partners[7:], partners[7:],
    )

    def hear(i):
        pl.semaphore_wait(ready.at[i], len(rounds[i]))

    def tell(i):
        if i:
            hear(i - 1)
        for partner in rounds[i]:
            pl.semaphore_signal(
                ready.at[i], inc=1, device_id=partner, device_id_type=MESH
            )

    low_lanes = lax.broadcasted_iota(jnp.int32, (32, 128), 1) < W

    def pair_up(first, second):
        return (
            jnp.where(low_lanes, first, pltpu.roll(second, W, 1)),
            jnp.where(low_lanes, pltpu.roll(first, W, 1), second),
        )

    def at(place):
        return place % 4 * 4 + place // 4

    def spread_amp(step, carry):
        p = (c // 2 + step) % 8
        for f in range(2):
            ci = 2 * p + f
            for a in range(32):
                flat[ci, pl.ds(a * N, N), :] = tin[ci, :, pl.ds(a * 128, 128)].astype(F32)
            for q in range(8):
                even, odd = pair_up(
                    flat[ci, pl.ds(at(2 * q), 32, stride=N), :],
                    flat[ci, pl.ds(at(2 * q + 1), 32, stride=N), :],
                )
                big[q, pl.ds(ci * W, 32, stride=2), :] = even
                big[q, pl.ds(ci * W + 1, 32, stride=2), :] = odd
        for q in range(8):
            block = big[q, pl.ds(pl.multiple_of(p * 128, 128), 128), :].T
            for g in range(2):
                first, second = pair_up(
                    block[g * W : g * W + 32], block[g * W + 32 : g * W + W]
                )
                tsend[2 * p * N + at(2 * q + g)] = first.astype(BF16)
                tsend[(2 * p + 1) * N + at(2 * q + g)] = second.astype(BF16)
        return carry

    def prepare(first, last):
        if first == 0:
            load_t.wait()
        lax.fori_loop(first, last, spread_amp, 0)
        if last == 8:
            own_tile.start()

    own_tile = pltpu.make_async_copy(
        tsend.at[c * N + r], trecv.at[c * N + r], own_sem
    )

    def send_tiles(dz, dl):
        def route(k, carry):
            rj = (y + k // 8) % 4 * 4 + (zh + dz) % 4
            ci = (x + k // 2) % 4 * 4 + (low // 2 + dl) % 2 * 2 + (low + k) % 2
            pltpu.make_async_remote_copy(
                src_ref=tsend.at[ci * N + rj], dst_ref=trecv.at[c * N + r],
                send_sem=tsend_sem, recv_sem=trecv_sem,
                device_id=(rj, ci), device_id_type=MESH,
            ).start()
            return carry

        lax.fori_loop(0 if dz or dl else 1, 32, route, 0)

    def own_z(h):
        if h == 0:
            load_right.wait()
        push_right(r, h, (down_z,))
        push_right(r, CHUNKS - 1 - h, (up_z,))

    def own_y():
        for h in range(CHUNKS):
            push_right(r, h, (up_y,))
            push_right(r, CHUNKS - 1 - h, (down_y,))

    def own_l():
        push_left(c, (zl_c,))

    def own_sib():
        load_left.wait()
        push_left(c, (sib,))

    def own_x():
        push_left(c, (cols(1), cols(-1), cols(2)))

    def pass_zl():
        got_left(zl_c)
        push_left(zl_c, (sib, cols(1), cols(-1), cols(2)))

    def pass_z(h):
        for slot, on, part in ((up_z, down_z, h), (down_z, up_z, CHUNKS - 1 - h)):
            got_right(slot, part)
            passed = (on,) if h < CHUNKS // 2 else ()
            push_right(slot, part, passed + (up_y, down_y))

    def pass_z2(h):
        got_right(far_z, h)
        push_right(far_z, h, (up_y, down_y))

    def pass_y(dz, h):
        for slot, on, part in (
            (rows(-1, dz), up_y, h), (rows(1, dz), down_y, CHUNKS - 1 - h),
        ):
            got_right(slot, part)
            push_right(slot, part, (on,))

    other_zl = 2 - 4 * (low // 2)

    def pass_x(dx, zl):
        slot = cols(dx) + zl * other_zl
        got_left(slot)
        push_left(slot, (sib,))

    def linear(step, carry):
        for f in range(4):
            ci = step * 4 + f
            for q in range(8):
                top, bottom = pair_up(
                    trecv[ci * N + at(2 * q)].astype(F32),
                    trecv[ci * N + at(2 * q + 1)].astype(F32),
                )
                span = pl.ds(pl.multiple_of(ci * W, W), 32)
                big[q, span, :] = big[q, span, :] + top
                span = pl.ds(pl.multiple_of(ci * W + 32, 32), 32)
                big[q, span, :] = big[q, span, :] + bottom
        span = pl.ds(pl.multiple_of(step * 256, 256), 256)
        which = lax.broadcasted_iota(jnp.int32, (256, 256), 0) // W
        first_e = jnp.zeros((256, 256), F32)
        for f in range(4):
            first_e = jnp.where(which == f, occ[r * N + step * 4 + f], first_e)
        which = lax.broadcasted_iota(jnp.int32, (256, 256), 1) // W
        for g in range(4):
            s = jnp.concatenate([big[2 * g, span, :], big[2 * g + 1, span, :]], axis=1)
            energy = first_e
            for f in range(4):
                energy = energy + jnp.where(which == f, occ[at(4 * g + f) * N + c], 0.0)
            sb = s.astype(BF16)
            total = jnp.dot(diag[...], sb, preferred_element_type=F32)
            total = total + lax.dot_general(sb, diag[...], NT, preferred_element_type=F32)
            total = total - energy * s
            big[2 * g, span, :] = total[:, :128]
            big[2 * g + 1, span, :] = total[:, 128:]
        return carry

    def mirrors():
        own_tile.wait()
        pltpu.make_async_copy(
            tsend.at[pl.ds(0, N * N - 1)], trecv.at[pl.ds(0, N * N - 1)], trecv_sem
        ).wait()
        lax.fori_loop(0, 4, linear, 0)

    def all_left():
        for xs in range(4):
            for b in range(2):
                got_left(xs * 4 + b * 2 + 1 - c % 2)

    def multiply(step, g):
        lhs = left[pl.ds(step * 8, 8)].reshape(512, 4096)
        rhs = right[pl.ds(pl.multiple_of(g * 4, 4), 4)].reshape(256, 4096)
        exch = lax.dot_general(lhs, rhs, NT, preferred_element_type=F32)
        return 2.0 * exch[:, :128], 2.0 * exch[:, 128:]

    def place(step, g):
        for f in range(8):
            ci = step * 8 + f
            for q in range(2):
                pair = pair_up(
                    big[2 * g + q, pl.ds(ci * W, 32, stride=2), :],
                    big[2 * g + q, pl.ds(ci * W + 1, 32, stride=2), :],
                )
                for tile, ys in zip(pair, (2 * q, 2 * q + 1)):
                    rj = ys * 4 + g
                    flat[ci, pl.ds(rj, 32, stride=N), :] = tile * flags[ci, rj].astype(F32)

    def arrived(dz):
        for h in range(CHUNKS):
            got_right(rows(1 if h < CHUNKS // 2 else -1, dz), h)
            got_right(rows(2, dz), h)

    def exchange(dz):
        g = (zh + dz + 4) % 4
        arrived(dz)

        def part(step, carry):
            span = pl.ds(pl.multiple_of(step * 512, 512), 512)
            acc[2 * g, span, :], acc[2 * g + 1, span, :] = multiply(step, g)
            return carry

        lax.fori_loop(0, 2, part, 0)

    def settle(dz):
        g = (zh + dz + 4) % 4

        def part(step, carry):
            span = pl.ds(pl.multiple_of(step * 512, 512), 512)
            for q in range(2):
                big[2 * g + q, span, :] = big[2 * g + q, span, :] + acc[2 * g + q, span, :]
            place(step, g)
            return carry

        lax.fori_loop(0, 2, part, 0)

    def last(dz):
        g = (zh + dz + 4) % 4
        arrived(dz)

        def part(step, carry):
            span = pl.ds(pl.multiple_of(step * 512, 512), 512)
            for q, x in enumerate(multiply(step, g)):
                big[2 * g + q, span, :] = big[2 * g + q, span, :] + x
            place(step, g)
            for f in range(8):
                ci = step * 8 + f
                for a in range(32):
                    obuf[ci, :, pl.ds(a * 128, 128)] = flat[ci, pl.ds(a * N, N), :].astype(BF16)
            return carry

        part(0, 0)
        part(1, 0)

    for cp in small:
        cp.wait()

    spread = (
        lax.broadcasted_iota(jnp.int32, (256, W), 0) % W
        == lax.broadcasted_iota(jnp.int32, (256, W), 1)
    ).astype(BF16)
    wide = jnp.dot(spread, fock[...], preferred_element_type=F32).astype(BF16)
    wide = lax.dot_general(wide, spread, NT, preferred_element_type=F32)
    same = (
        lax.broadcasted_iota(jnp.int32, (256, 256), 0) // W
        == lax.broadcasted_iota(jnp.int32, (256, 256), 1) // W
    )
    diag[...] = jnp.where(same, wide, 0.0).astype(BF16)

    steps = {
        "Y": own_y, "S": own_sib, "L": own_l, "X": own_x, "zl": pass_zl, "ready": lambda: hear(5),
        "x1": lambda: (pass_x(1, 0), pass_x(-1, 0)), "x2": lambda: pass_x(2, 0),
        "x3": lambda: (pass_x(1, 1), pass_x(-1, 1)), "x4": lambda: pass_x(2, 1),
        "left": all_left, "lin": mirrors,
    }
    numbered = {
        "Z": own_z, "z": pass_z, "f": pass_z2, "y": pass_y, "T": send_tiles,
        "p": prepare, "g": tell,
        "m": exchange, "s": settle, "e": last,
    }
    for name in PLAN:
        if name in steps:
            steps[name]()
        else:
            numbered[name[0]](*(int(digit) for digit in name[1:]))

    for cp in started:
        cp.wait_send()
    pltpu.make_async_copy(
        tsend.at[pl.ds(0, N * N - 1)], trecv.at[pl.ds(0, N * N - 1)], tsend_sem
    ).wait()


def put_out(held, out, sem):
    copies = [pltpu.make_async_copy(held.at[i], out.at[i], sem.at[i]) for i in range(N)]
    for copy in copies:
        copy.start()
    for copy in copies:
        copy.wait()


def shards(amplitudes, panels, fock_virt, occ_energy, strong_pairs):
    naux = panels.shape[2]
    hbm = pl.BlockSpec(memory_space=pltpu.HBM)
    vmem = pl.BlockSpec(memory_space=pltpu.VMEM)
    dma = pltpu.SemaphoreType.DMA
    result = pl.pallas_call(
        kernel,
        out_shape=pltpu.VMEM((N, N, W * W), BF16),
        in_specs=[hbm] * 5,
        out_specs=vmem,
        scratch_shapes=[
            pltpu.VMEM((N, W, naux), BF16),
            pltpu.VMEM((N, W, naux), BF16),
            pltpu.VMEM((N, N, W * W), BF16),
            pltpu.VMEM((N * N, 32, 128), BF16),
            pltpu.VMEM((N * N, 32, 128), BF16),
            pltpu.VMEM((8, N * W, 128), F32),
            pltpu.VMEM((8, N * W, 128), F32),
            pltpu.VMEM((N, 32 * N, 128), F32),
            pltpu.VMEM((256, 256), BF16),
            pltpu.VMEM((W, W), BF16),
            pltpu.SMEM((N * N,), F32),
            pltpu.SMEM((N, N), jnp.int32),
            dma((2,)),
            dma,
            dma((3,)),
            dma,
            dma,
            dma,
            dma((16,)),
            dma((N,)),
            dma((64,)),
            dma((N, CHUNKS)),
            pltpu.SemaphoreType.REGULAR((6,)),
        ],
        compiler_params=pltpu.CompilerParams(
            collective_id=0, has_side_effects=True, vmem_limit_bytes=56 * 2**20
        ),
        name="residual",
    )(
        amplitudes.reshape(N, N, W * W),
        panels,
        fock_virt,
        occ_energy,
        strong_pairs.reshape(N, N),
    )
    result = pl.pallas_call(
        put_out,
        out_shape=jax.ShapeDtypeStruct((N, N, W * W), BF16),
        in_specs=[pl.BlockSpec(memory_space=pltpu.VMEM)],
        out_specs=pl.BlockSpec(memory_space=pltpu.HBM),
        scratch_shapes=[dma((N,))],
        compiler_params=pltpu.CompilerParams(vmem_limit_bytes=2**20),
        name="put_out",
    )(result)
    return result.reshape(amplitudes.shape)


def solution(mesh):
    placed = (
        P("row", None, None, None, "col", None, None),
        P(("row", "col"), None, None),
        P(),
        P(),
        P("row", None, None, None, "col", None),
    )
    return jax.shard_map(
        shards,
        mesh=mesh,
        in_specs=placed,
        out_specs=P("row", None, None, None, "col", None, None),
        check_vma=False,
    )
```

```python
import jax
import jax.numpy as jnp
from jax import lax
from jax.experimental import pallas as pl
from jax.experimental.pallas import tpu as pltpu
from jax.sharding import PartitionSpec as P

MESH = pl.DeviceIdType.MESH
F32 = jnp.float32
BF16 = jnp.bfloat16
N = 16
W = 64
NT = (((1,), (1,)), ((), ()))
PLAN = (
    "Z0", "Z1", "Y", "S", "L", "X", "g0", "p04", "g1", "p48", "g2", "g3", "g4", "g5", "ready",
    "T00", "y00", "z0", "z1", "zl", "T01", "T10", "f0", "T11", "T30", "f1", "T31", "T20", "y10",
    "T21", "y30", "x1", "x2", "x3", "x4", "left", "m0", "y20", "m1", "m3", "lin", "s013", "e2",
)
CHUNKS = 2


def kernel(
    amp, panel, fock_in, occ_in, flags_in, obuf,
    left, right, tin, tsend, trecv, big, acc, flat, diag, fock, occ, flags,
    psem, tsem, small_sem, tsend_sem, trecv_sem, own_sem,
    lsend, lrecv, rsend, rrecv, ready,
):
    r = lax.axis_index("row")
    c = lax.axis_index("col")
    y, zh = r // 4, r % 4
    x, low = c // 4, c % 4

    def rows(dy, dz):
        return (y + dy + 4) % 4 * 4 + (zh + dz + 4) % 4

    def cols(dx):
        return (x + dx + 4) % 4 * 4 + low

    sib = c + 1 - 2 * (c % 2)
    zl_c = c + 2 - 4 * (low // 2)

    bar = pltpu.get_barrier_semaphore()

    partners = [(r, col) for col in (sib, zl_c, cols(1), cols(-1), cols(2))]
    partners += [(row, c) for row in (rows(0, 1), rows(0, -1), rows(1, 0), rows(-1, 0))]
    for partner in partners:
        pl.semaphore_signal(bar, inc=1, device_id=partner, device_id_type=MESH)

    load_left = pltpu.make_async_copy(panel.at[0], left.at[c], psem.at[0])
    load_right = pltpu.make_async_copy(panel.at[0], right.at[zh * 4 + y], psem.at[1])
    load_t = pltpu.make_async_copy(amp, tin, tsem)
    load_right.start()
    load_left.start()
    load_t.start()
    small = [
        pltpu.make_async_copy(src, dst, small_sem.at[i])
        for i, (src, dst) in enumerate(((fock_in, fock), (occ_in, occ), (flags_in, flags)))
    ]
    for cp in small:
        cp.start()
    pl.semaphore_wait(bar, len(partners))

    started = []

    def send_left(slot, col, k):
        cp = pltpu.make_async_remote_copy(
            src_ref=left.at[slot], dst_ref=left.at[slot],
            send_sem=lsend.at[k], recv_sem=lrecv.at[slot],
            device_id=(r, col), device_id_type=MESH,
        )
        cp.start()
        started.append(cp)

    def got_left(slot):
        pltpu.make_async_remote_copy(
            src_ref=left.at[slot], dst_ref=left.at[slot],
            send_sem=lsend.at[0], recv_sem=lrecv.at[slot],
            device_id=(r, sib), device_id_type=MESH,
        ).wait_recv()

    def half(slot, h):
        return right.at[slot % 4 * 4 + slot // 4, pl.ds(h * (W // CHUNKS), W // CHUNKS)]

    def send_right(slot, h, row, k):
        cp = pltpu.make_async_remote_copy(
            src_ref=half(slot, h), dst_ref=half(slot, h),
            send_sem=rsend.at[k], recv_sem=rrecv.at[slot, h],
            device_id=(row, c), device_id_type=MESH,
        )
        cp.start()
        started.append(cp)

    def got_right(slot, h):
        pltpu.make_async_remote_copy(
            src_ref=half(slot, h), dst_ref=half(slot, h),
            send_sem=rsend.at[0], recv_sem=rrecv.at[slot, h],
            device_id=(rows(1, 0), c), device_id_type=MESH,
        ).wait_recv()

    up_z, down_z, far_z = rows(0, 1), rows(0, -1), rows(0, 2)
    up_y, down_y = rows(1, 0), rows(-1, 0)
    next_left, next_right = iter(range(16)), iter(range(64))

    def push_left(slot, cols_to):
        for col in cols_to:
            send_left(slot, col, next(next_left))

    def push_right(slot, h, rows_to):
        for row in rows_to:
            send_right(slot, h, row, next(next_right))

    rounds = (
        (partners[0],), (partners[1],), partners[5:7], partners[5:7], partners[7:], partners[7:],
    )

    def hear(i):
        pl.semaphore_wait(ready.at[i], len(rounds[i]))

    def tell(i):
        if i:
            hear(i - 1)
        for partner in rounds[i]:
            pl.semaphore_signal(
                ready.at[i], inc=1, device_id=partner, device_id_type=MESH
            )

    low_lanes = lax.broadcasted_iota(jnp.int32, (32, 128), 1) < W

    def pair_up(first, second):
        return (
            jnp.where(low_lanes, first, pltpu.roll(second, W, 1)),
            jnp.where(low_lanes, pltpu.roll(first, W, 1), second),
        )

    def at(place):
        return place % 4 * 4 + place // 4

    def spread_amp(step, carry):
        p = (c // 2 + step) % 8
        for f in range(2):
            ci = 2 * p + f
            for a in range(32):
                flat[ci, pl.ds(a * N, N), :] = tin[ci, :, pl.ds(a * 128, 128)].astype(F32)
            for q in range(8):
                even, odd = pair_up(
                    flat[ci, pl.ds(at(2 * q), 32, stride=N), :],
                    flat[ci, pl.ds(at(2 * q + 1), 32, stride=N), :],
                )
                big[q, pl.ds(ci * W, 32, stride=2), :] = even
                big[q, pl.ds(ci * W + 1, 32, stride=2), :] = odd
        for q in range(8):
            block = big[q, pl.ds(pl.multiple_of(p * 128, 128), 128), :].T
            for g in range(2):
                first, second = pair_up(
                    block[g * W : g * W + 32], block[g * W + 32 : g * W + W]
                )
                tsend[2 * p * N + at(2 * q + g)] = first.astype(BF16)
                tsend[(2 * p + 1) * N + at(2 * q + g)] = second.astype(BF16)
        return carry

    def prepare(first, last):
        if first == 0:
            load_t.wait()
        lax.fori_loop(first, last, spread_amp, 0)
        if last == 8:
            own_tile.start()

    own_tile = pltpu.make_async_copy(
        tsend.at[c * N + r], trecv.at[c * N + r], own_sem
    )

    def send_tiles(dz, dl):
        def route(k, carry):
            rj = (y + k // 8) % 4 * 4 + (zh + dz) % 4
            ci = (x + k // 2) % 4 * 4 + (low // 2 + dl) % 2 * 2 + (low + k) % 2
            pltpu.make_async_remote_copy(
                src_ref=tsend.at[ci * N + rj], dst_ref=trecv.at[c * N + r],
                send_sem=tsend_sem, recv_sem=trecv_sem,
                device_id=(rj, ci), device_id_type=MESH,
            ).start()
            return carry

        lax.fori_loop(0 if dz or dl else 1, 32, route, 0)

    def own_z(h):
        if h == 0:
            load_right.wait()
        push_right(r, h, (down_z,))
        push_right(r, CHUNKS - 1 - h, (up_z,))

    def own_y():
        for h in range(CHUNKS):
            push_right(r, h, (up_y,))
            push_right(r, CHUNKS - 1 - h, (down_y,))

    def own_l():
        push_left(c, (zl_c,))

    def own_sib():
        load_left.wait()
        push_left(c, (sib,))

    def own_x():
        push_left(c, (cols(1), cols(-1), cols(2)))

    def pass_zl():
        got_left(zl_c)
        push_left(zl_c, (sib, cols(1), cols(-1), cols(2)))

    def pass_z(h):
        for slot, on, part in ((up_z, down_z, h), (down_z, up_z, CHUNKS - 1 - h)):
            got_right(slot, part)
            passed = (on,) if h < CHUNKS // 2 else ()
            push_right(slot, part, passed + (up_y, down_y))

    def pass_z2(h):
        got_right(far_z, h)
        push_right(far_z, h, (up_y, down_y))

    def pass_y(dz, h):
        for slot, on, part in (
            (rows(-1, dz), up_y, h), (rows(1, dz), down_y, CHUNKS - 1 - h),
        ):
            got_right(slot, part)
            push_right(slot, part, (on,))

    other_zl = 2 - 4 * (low // 2)

    def pass_x(dx, zl):
        slot = cols(dx) + zl * other_zl
        got_left(slot)
        push_left(slot, (sib,))

    def linear(step, carry):
        for f in range(4):
            ci = step * 4 + f
            for q in range(8):
                top, bottom = pair_up(
                    trecv[ci * N + at(2 * q)].astype(F32),
                    trecv[ci * N + at(2 * q + 1)].astype(F32),
                )
                span = pl.ds(pl.multiple_of(ci * W, W), 32)
                big[q, span, :] = big[q, span, :] + top
                span = pl.ds(pl.multiple_of(ci * W + 32, 32), 32)
                big[q, span, :] = big[q, span, :] + bottom
        span = pl.ds(pl.multiple_of(step * 256, 256), 256)
        which = lax.broadcasted_iota(jnp.int32, (256, 256), 0) // W
        first_e = jnp.zeros((256, 256), F32)
        for f in range(4):
            first_e = jnp.where(which == f, occ[r * N + step * 4 + f], first_e)
        which = lax.broadcasted_iota(jnp.int32, (256, 256), 1) // W
        for g in range(4):
            s = jnp.concatenate([big[2 * g, span, :], big[2 * g + 1, span, :]], axis=1)
            energy = first_e
            for f in range(4):
                energy = energy + jnp.where(which == f, occ[at(4 * g + f) * N + c], 0.0)
            sb = s.astype(BF16)
            total = jnp.dot(diag[...], sb, preferred_element_type=F32)
            total = total + lax.dot_general(sb, diag[...], NT, preferred_element_type=F32)
            total = total - energy * s
            big[2 * g, span, :] = total[:, :128]
            big[2 * g + 1, span, :] = total[:, 128:]
        return carry

    def mirrors():
        own_tile.wait()
        pltpu.make_async_copy(
            tsend.at[pl.ds(0, N * N - 1)], trecv.at[pl.ds(0, N * N - 1)], trecv_sem
        ).wait()
        lax.fori_loop(0, 4, linear, 0)

    def all_left():
        for xs in range(4):
            for b in range(2):
                got_left(xs * 4 + b * 2 + 1 - c % 2)

    def multiply(step, g):
        lhs = left[pl.ds(step * 8, 8)].reshape(512, 4096)
        rhs = right[pl.ds(pl.multiple_of(g * 4, 4), 4)].reshape(256, 4096)
        exch = lax.dot_general(lhs, rhs, NT, preferred_element_type=F32)
        return 2.0 * exch[:, :128], 2.0 * exch[:, 128:]

    def place(step, g):
        for f in range(8):
            ci = step * 8 + f
            for q in range(2):
                pair = pair_up(
                    big[2 * g + q, pl.ds(ci * W, 32, stride=2), :],
                    big[2 * g + q, pl.ds(ci * W + 1, 32, stride=2), :],
                )
                for tile, ys in zip(pair, (2 * q, 2 * q + 1)):
                    rj = ys * 4 + g
                    flat[ci, pl.ds(rj, 32, stride=N), :] = tile * flags[ci, rj].astype(F32)

    def arrived(dz):
        for h in range(CHUNKS):
            got_right(rows(1 if h < CHUNKS // 2 else -1, dz), h)
            got_right(rows(2, dz), h)

    def exchange(dz):
        g = (zh + dz + 4) % 4
        arrived(dz)

        def part(step, carry):
            span = pl.ds(pl.multiple_of(step * 512, 512), 512)
            acc[2 * g, span, :], acc[2 * g + 1, span, :] = multiply(step, g)
            return carry

        lax.fori_loop(0, 2, part, 0)

    def settle(*steps_z):
        def part(step, carry):
            span = pl.ds(pl.multiple_of(step * 512, 512), 512)
            for dz in steps_z:
                g = (zh + dz + 4) % 4
                for q in range(2):
                    big[2 * g + q, span, :] = big[2 * g + q, span, :] + acc[2 * g + q, span, :]
                place(step, g)
            return carry

        lax.fori_loop(0, 2, part, 0)

    def last(dz):
        g = (zh + dz + 4) % 4
        arrived(dz)

        def part(step, carry):
            span = pl.ds(pl.multiple_of(step * 512, 512), 512)
            for q, x in enumerate(multiply(step, g)):
                big[2 * g + q, span, :] = big[2 * g + q, span, :] + x
            place(step, g)
            for f in range(8):
                ci = step * 8 + f
                for a in range(32):
                    obuf[ci, :, pl.ds(a * 128, 128)] = flat[ci, pl.ds(a * N, N), :].astype(BF16)
            return carry

        part(0, 0)
        part(1, 0)

    for cp in small:
        cp.wait()

    spread = (
        lax.broadcasted_iota(jnp.int32, (256, W), 0) % W
        == lax.broadcasted_iota(jnp.int32, (256, W), 1)
    ).astype(BF16)
    wide = jnp.dot(spread, fock[...], preferred_element_type=F32).astype(BF16)
    wide = lax.dot_general(wide, spread, NT, preferred_element_type=F32)
    same = (
        lax.broadcasted_iota(jnp.int32, (256, 256), 0) // W
        == lax.broadcasted_iota(jnp.int32, (256, 256), 1) // W
    )
    diag[...] = jnp.where(same, wide, 0.0).astype(BF16)

    steps = {
        "Y": own_y, "S": own_sib, "L": own_l, "X": own_x, "zl": pass_zl, "ready": lambda: hear(5),
        "x1": lambda: (pass_x(1, 0), pass_x(-1, 0)), "x2": lambda: pass_x(2, 0),
        "x3": lambda: (pass_x(1, 1), pass_x(-1, 1)), "x4": lambda: pass_x(2, 1),
        "left": all_left, "lin": mirrors,
    }
    numbered = {
        "Z": own_z, "z": pass_z, "f": pass_z2, "y": pass_y, "T": send_tiles,
        "p": prepare, "g": tell,
        "m": exchange, "s": settle, "e": last,
    }
    for name in PLAN:
        if name in steps:
            steps[name]()
        else:
            numbered[name[0]](*(int(digit) for digit in name[1:]))

    for cp in started:
        cp.wait_send()
    pltpu.make_async_copy(
        tsend.at[pl.ds(0, N * N - 1)], trecv.at[pl.ds(0, N * N - 1)], tsend_sem
    ).wait()


def put_out(held, out, sem):
    copies = [pltpu.make_async_copy(held.at[i], out.at[i], sem.at[i]) for i in range(N)]
    for copy in copies:
        copy.start()
    for copy in copies:
        copy.wait()


def shards(amplitudes, panels, fock_virt, occ_energy, strong_pairs):
    naux = panels.shape[2]
    hbm = pl.BlockSpec(memory_space=pltpu.HBM)
    vmem = pl.BlockSpec(memory_space=pltpu.VMEM)
    dma = pltpu.SemaphoreType.DMA
    result = pl.pallas_call(
        kernel,
        out_shape=pltpu.VMEM((N, N, W * W), BF16),
        in_specs=[hbm] * 5,
        out_specs=vmem,
        scratch_shapes=[
            pltpu.VMEM((N, W, naux), BF16),
            pltpu.VMEM((N, W, naux), BF16),
            pltpu.VMEM((N, N, W * W), BF16),
            pltpu.VMEM((N * N, 32, 128), BF16),
            pltpu.VMEM((N * N, 32, 128), BF16),
            pltpu.VMEM((8, N * W, 128), F32),
            pltpu.VMEM((8, N * W, 128), F32),
            pltpu.VMEM((N, 32 * N, 128), F32),
            pltpu.VMEM((256, 256), BF16),
            pltpu.VMEM((W, W), BF16),
            pltpu.SMEM((N * N,), F32),
            pltpu.SMEM((N, N), jnp.int32),
            dma((2,)),
            dma,
            dma((3,)),
            dma,
            dma,
            dma,
            dma((16,)),
            dma((N,)),
            dma((64,)),
            dma((N, CHUNKS)),
            pltpu.SemaphoreType.REGULAR((6,)),
        ],
        compiler_params=pltpu.CompilerParams(
            collective_id=0, has_side_effects=True, vmem_limit_bytes=56 * 2**20
        ),
        name="residual",
    )(
        amplitudes.reshape(N, N, W * W),
        panels,
        fock_virt,
        occ_energy,
        strong_pairs.reshape(N, N),
    )
    result = pl.pallas_call(
        put_out,
        out_shape=jax.ShapeDtypeStruct((N, N, W * W), BF16),
        in_specs=[pl.BlockSpec(memory_space=pltpu.VMEM)],
        out_specs=pl.BlockSpec(memory_space=pltpu.HBM),
        scratch_shapes=[dma((N,))],
        compiler_params=pltpu.CompilerParams(vmem_limit_bytes=2**20),
        name="put_out",
    )(result)
    return result.reshape(amplitudes.shape)


def solution(mesh):
    placed = (
        P("row", None, None, None, "col", None, None),
        P(("row", "col"), None, None),
        P(),
        P(),
        P("row", None, None, None, "col", None),
    )
    return jax.shard_map(
        shards,
        mesh=mesh,
        in_specs=placed,
        out_specs=P("row", None, None, None, "col", None, None),
        check_vma=False,
    )
```
